256 devices in a mesh: rep: 32 (over z_lo, x, core), tp: 8 (over y, z_hi).
Axes of the slice: x: 4, y: 4, z: 8 (z_hi: 2, z_lo: 4; z = z_hi * 4 + z_lo), core: 2. Of those that a mesh axis runs over, the one named last changes fastest.
Arguments:
- prefix_hidden_states: bfloat16 [32, 768, 8192], P('rep', None, 'tp'), may hold values from -6 to 6
- latest_hidden: bfloat16 [1024, 8192], P('rep', 'tp'), may hold values from -6 to 6
- queries: bfloat16 [1024, 8192], P('rep', 'tp'), may hold values from -64 to 64
- suffix_key_cache: bfloat16 [1024, 128, 2048], P('rep', None, 'tp'), may hold values from -6 to 6
- key_value_weight: bfloat16 [8192, 2048], P('tp'), may hold values from -0.0625 to 0.0625
- key_value_bias: bfloat16 [2048], P('tp'), may hold values from -3 to 3
- adapter_down_weight: bfloat16 [8192, 512], P('tp'), may hold values from -0.0625 to 0.0625
- adapter_up_weight: bfloat16 [512, 1024], replicated, may hold values from -0.41992188 to 0.41992188
- parents: int32 [1024, 1], P('rep'), may hold values from 0 to 31; in each aligned block of 32 rows (0 to 31, 32 to 63, ...) at most 2 rows name the same one
- adapter_index: int32 [32], replicated, may hold values from 0 to 7
- suffix_length_count: int32 [1024], P('rep'), may hold values from 1 to 128, as said below
Outputs:
- prefix_kv: bfloat16 [32, 768, 2048], P('rep', None, 'tp')
- latest_key_value: bfloat16 [1024, 2048], P('rep', 'tp')
- attn_out: bfloat16 [1024, 8192], P('rep', 'tp')
The draws below stay inside these ranges and needn't reach their ends.
Inputs may be any that keep to these rules, and one draw needn't show every extreme that they name: `parents`: among the completions of one index of rep no prompt is named more than 2 times, and every prompt is named by some completion. The new token of completion c sits right after its suffix_length_count[c] cached tokens.
All inputs are finite; a program needn't handle non-finite values.
Results may differ from the reference program's by a relative error of at most 0.01005.
The reference program's roundings to bfloat16 on the way count: a program that leaves them out, or rounds other values in their place, can miss the bound.
Values may be sent and summed in bfloat16 or wider, within the bound.
No kernel may reach another device: no remote copies, remote signals or barrier semaphores. Data moves between devices by JAX's collectives and lax.ppermute only.
A program may use at most 128 MiB of HBM per device.

```python
import math
import jax
import jax.numpy as jnp
import numpy as np
from jax import lax

MODEL_WIDTH = 8192
Q_HEADS = 64
KEY_VALUE_HEADS = 8
HEAD_WIDTH = 128
ADAPTER_RANK = 32
ADAPTER_COUNT = 8
PREFIX_LENGTH = 768
SUF = 128
C_DEV = 32
CAP = 2
PROMPTS = 32
COMPLETION_COUNT = 1024


def draw_queries(key, part):
    key = jax.random.fold_in(key, 11)
    first_key = jax.random.fold_in(key, 0)
    shape_full = (COMPLETION_COUNT, Q_HEADS, HEAD_WIDTH)
    values = jnp.clip(1.5 * jax.random.normal(first_key, shape_full, jnp.float32), -6.0, 6.0)
    return values.reshape(COMPLETION_COUNT, Q_HEADS * HEAD_WIDTH).astype(jnp.bfloat16)


def draw_suffix_length_count(key, part):
    key = jax.random.fold_in(key, 23)
    first_key, second_key = jax.random.split(key)
    lengths = jax.random.randint(first_key, (COMPLETION_COUNT,), 1, SUF + 1, dtype=jnp.int32)
    marked = jax.random.randint(second_key, (), 0, COMPLETION_COUNT, dtype=jnp.int32)
    return jnp.where(jnp.arange(COMPLETION_COUNT, dtype=jnp.int32) == marked, SUF, lengths).astype(jnp.int32)


def place_ends(drawn, stream_key, smallest, high):
    place = [jax.random.randint(jax.random.fold_in(stream_key, axis), (), 0, length) for axis, length in enumerate(drawn.shape)]
    widest = drawn.shape.index(max(drawn.shape))
    next_to = place[:widest] + [(place[widest] + 1) % drawn.shape[widest]] + place[widest + 1:]
    return drawn.at[tuple(place)].set(smallest).at[tuple(next_to)].set(high)


def level_of(rng, extent, cuts, low, high):
    loudness = 1.0
    for position, parts in cuts:
        steps = jax.random.uniform(jax.random.fold_in(jax.random.fold_in(rng, 6), position), (parts,), jnp.float32, low / len(cuts), high / len(cuts))
        loudness = loudness * jnp.repeat(jnp.exp(steps), extent[position] // parts).reshape((-1,) + (1,) * (len(extent) - 1 - position))
    return loudness


def routed_block(rng, own, number, rows, amount, top, most, slope):
    ranking = jax.random.permutation(rng, amount)
    packed, common = portions_of(amount, rows * top, most, slope, True), portions_of(amount, rows * top, most, slope, False)
    places = jnp.arange(amount)

    def named(tallies, offset_by):
        used = int((tallies > 0).sum())
        fixed = max(1, used // 4)
        passed = fixed + (places - fixed + offset_by * (used - fixed)) % max(1, amount - fixed)
        return jnp.zeros((amount,), jnp.int32).at[ranking[jnp.where(places < fixed, places, passed)]].set(jnp.asarray(tallies, jnp.int32))

    tallies = jnp.where(number % 4 == 0, named(packed, number // 4), named(common, number - number // 4 - 1))
    mixed = jax.random.permutation(jax.random.fold_in(own, 3), amount)
    donor, taker = mixed[0:amount // 2 * 2:2], mixed[1:amount // 2 * 2:2]
    room = jnp.minimum(tallies[donor] - 1, most - tallies[taker]) // 2
    room = jnp.where((donor == ranking[0]) | (taker == ranking[0]) | (tallies[taker] == 0), 0, jnp.maximum(room, 0))
    passed = jax.random.randint(jax.random.fold_in(own, 4), (amount // 2,), 0, 1 << 20) % (room + 1)
    tallies = tallies.at[donor].add(-passed).at[taker].add(passed)
    items = jnp.searchsorted(jnp.cumsum(tallies), jnp.arange(rows * top), side="right").astype(jnp.int32)
    grid = items.reshape(top, rows).T
    grid = grid[jax.random.permutation(jax.random.fold_in(own, 1), rows)]
    offset_by = jax.random.randint(jax.random.fold_in(own, 2), (rows, 1), 0, top)
    return jnp.take_along_axis(grid, (jnp.arange(top)[None, :] + offset_by) % top, axis=1)


def portions_of(number_of, total, most, skew, full):
    loads = [(1 << 20) // math.isqrt(rank ** skew) + 1 for rank in range(1, number_of + 1)]
    largest = most if full else min(most, max(-(-total // number_of), total * loads[0] // sum(loads)))
    least = 1 if total - largest >= number_of - 1 else 0
    holding, spare = [largest] + [least] * (number_of - 1), total - largest - least * (number_of - 1)
    while spare > 0:
        candidates = [i for i in range(1, number_of) if holding[i] < largest] or [i for i in range(1, number_of) if holding[i] < most]
        whole, left = sum([loads[i] for i in candidates]), spare
        for i in candidates:
            more = min(most - holding[i], max(1, left * loads[i] // whole), spare)
            holding[i] = holding[i] + more
            spare = spare - more
    return np.array(holding)


def scatter_about(stream_key, extent, width, limit, cuts=(), kind=jnp.bfloat16):
    values = jax.random.normal(stream_key, extent, jnp.float32) * width
    if len(cuts) > 0:
        values = level_of(stream_key, extent, cuts, -0.22, 0.18) * values
    return jnp.clip(values, min=-limit, max=limit).astype(kind)


def setup_inputs(seed: int = 0) -> dict:
    key_of = jax.random.split(jax.random.key(seed), 12)
    prefix_hidden_states = scatter_about(key_of[0], (PROMPTS, PREFIX_LENGTH, MODEL_WIDTH), 1.0, 6.0, ((0, 32), (2, 8)))
    latest_hidden = scatter_about(key_of[1], (COMPLETION_COUNT, MODEL_WIDTH), 1.0, 6.0, ((0, 32), (1, 8)))
    queries = draw_queries(jax.random.fold_in(key_of[11], 71), 0)
    suffix_key_cache = scatter_about(key_of[3], (COMPLETION_COUNT, SUF, KEY_VALUE_HEADS * 2 * HEAD_WIDTH), 1.0, 6.0, ((0, 32), (2, 8)))
    key_value_weight = scatter_about(key_of[4], (MODEL_WIDTH, KEY_VALUE_HEADS * 2 * HEAD_WIDTH), MODEL_WIDTH ** -0.5, 0.0625, ((0, 8),))
    key_value_bias = scatter_about(key_of[5], (KEY_VALUE_HEADS * 2 * HEAD_WIDTH,), 0.5, 3.0, ((0, 8),))
    adapter_down_weight = scatter_about(key_of[6], (MODEL_WIDTH, ADAPTER_COUNT * 2 * ADAPTER_RANK), MODEL_WIDTH ** -0.5, 0.0625, ((0, 8),))
    adapter_up_weight = scatter_about(key_of[7], (ADAPTER_COUNT * 2 * ADAPTER_RANK, KEY_VALUE_HEADS * HEAD_WIDTH), 0.07, 0.41992188)
    parents_keys = jax.random.split(jax.random.fold_in(key_of[8], 1), COMPLETION_COUNT // C_DEV)
    parents_turns = jax.random.permutation(jax.random.fold_in(key_of[8], 3), COMPLETION_COUNT // C_DEV)
    parents = jax.vmap(lambda own, number: routed_block(jax.random.fold_in(key_of[8], 2), own, number, C_DEV, PROMPTS, 1, CAP, 2))(parents_keys, parents_turns).reshape((COMPLETION_COUNT, 1))
    adapter_index = place_ends(jax.random.randint(key_of[9], (PROMPTS,), 0, ADAPTER_COUNT), jax.random.fold_in(key_of[9], 1), 0, ADAPTER_COUNT - 1).astype(jnp.int32)
    suffix_length_count = draw_suffix_length_count(jax.random.fold_in(key_of[11], 71), 0)
    return dict(prefix_hidden_states=prefix_hidden_states, latest_hidden=latest_hidden, queries=queries, suffix_key_cache=suffix_key_cache, key_value_weight=key_value_weight, key_value_bias=key_value_bias, adapter_down_weight=adapter_down_weight, adapter_up_weight=adapter_up_weight, parents=parents, adapter_index=adapter_index, suffix_length_count=suffix_length_count)


rope_base = 1000000.0
neg_fill = -1.0e30


def rotate(values, token_position):
    half_dim = values.shape[-1] // 2
    frequency = rope_base ** (-(jnp.arange(half_dim, dtype=jnp.float32) * 2.0) / values.shape[-1])
    angles = token_position.astype(jnp.float32)[:, None] * frequency[None, :]
    cosine = jnp.cos(angles)[:, None, :]
    sine_wave = jnp.sin(angles)[:, None, :]
    first_half = values[..., :half_dim]
    second_half = values[..., half_dim:]
    return jnp.concatenate([first_half * cosine - second_half * sine_wave, second_half * cosine + first_half * sine_wave], axis=-1)


def project_rows(hidden_state, rank_products, selector_mask, token_position, key_value_weight, key_value_bias, adapter_up_weight):
    row_count = hidden_state.shape[0]
    base_part = jnp.dot(hidden_state, key_value_weight, preferred_element_type=jnp.float32)
    up_weight_all = adapter_up_weight.astype(jnp.float32).reshape(ADAPTER_COUNT, 2, ADAPTER_RANK, KEY_VALUE_HEADS * HEAD_WIDTH)
    masked = selector_mask[:, :, None, None] * rank_products.reshape(row_count, 1, 2, ADAPTER_RANK)
    delta_key = jnp.dot(masked[:, :, 0, :].reshape(row_count, ADAPTER_COUNT * ADAPTER_RANK), up_weight_all[:, 0].reshape(ADAPTER_COUNT * ADAPTER_RANK, KEY_VALUE_HEADS * HEAD_WIDTH), precision=lax.Precision.HIGHEST)
    delta_value = jnp.dot(masked[:, :, 1, :].reshape(row_count, ADAPTER_COUNT * ADAPTER_RANK), up_weight_all[:, 1].reshape(ADAPTER_COUNT * ADAPTER_RANK, KEY_VALUE_HEADS * HEAD_WIDTH), precision=lax.Precision.HIGHEST)
    shaped = base_part.reshape(row_count, KEY_VALUE_HEADS, 2, HEAD_WIDTH) + key_value_bias.astype(jnp.float32).reshape(KEY_VALUE_HEADS, 2, HEAD_WIDTH)
    shaped = shaped + jnp.stack([delta_key.reshape(row_count, KEY_VALUE_HEADS, HEAD_WIDTH), delta_value.reshape(row_count, KEY_VALUE_HEADS, HEAD_WIDTH)], axis=2)
    key_part = rotate(shaped[:, :, 0], token_position)
    return jnp.stack([key_part, shaped[:, :, 1]], axis=2).reshape(row_count, KEY_VALUE_HEADS * 2 * HEAD_WIDTH).astype(jnp.bfloat16)


def attend(query_rot, key_part, value_part, valid_mask):
    scores = jnp.einsum("gqd,ngd->gqn", query_rot.astype(jnp.float32), key_part.astype(jnp.float32)) * (HEAD_WIDTH ** -0.5)
    scores = jnp.where(valid_mask[None, None, :], scores, neg_fill)
    top_score = jnp.max(scores, axis=-1)
    weights_f = jnp.exp(scores - top_score[..., None])
    total_sum = jnp.sum(weights_f, axis=-1)
    rounded = lax.optimization_barrier(weights_f.astype(jnp.bfloat16)).astype(jnp.float32)
    out_part = jnp.einsum("gqn,ngd->gqd", rounded, value_part.astype(jnp.float32))
    return out_part, top_score, total_sum


def reference(prefix_hidden_states, latest_hidden, queries, suffix_key_cache, key_value_weight, key_value_bias, adapter_down_weight, adapter_up_weight, parents, adapter_index, suffix_length_count):
    adapter_range = jnp.arange(ADAPTER_COUNT, dtype=jnp.int32)

    def one_prompt(item_args):
        hidden_state, adapter_slot = item_args
        down_columns = lax.dynamic_slice_in_dim(adapter_down_weight, adapter_slot * (2 * ADAPTER_RANK), 2 * ADAPTER_RANK, 1)
        rank_products = jnp.dot(hidden_state, down_columns, preferred_element_type=jnp.float32)
        selector_mask = jnp.broadcast_to((adapter_range == adapter_slot).astype(jnp.float32)[None, :], (PREFIX_LENGTH, ADAPTER_COUNT))
        return project_rows(hidden_state, rank_products, selector_mask, jnp.arange(PREFIX_LENGTH, dtype=jnp.int32), key_value_weight, key_value_bias, adapter_up_weight)

    prefix_kv = lax.map(one_prompt, (prefix_hidden_states, adapter_index))
    parent = parents[:, 0]
    new_adapter = adapter_index[parent]
    selector_mask = (new_adapter[:, None] == adapter_range[None, :]).astype(jnp.float32)
    down_weight_all = jnp.dot(latest_hidden, adapter_down_weight, preferred_element_type=jnp.float32).reshape(COMPLETION_COUNT, ADAPTER_COUNT, 2 * ADAPTER_RANK)
    rank_latest = jnp.sum(selector_mask[:, :, None] * down_weight_all, axis=1)
    token_position = PREFIX_LENGTH + suffix_length_count
    latest_key_value = project_rows(latest_hidden, rank_latest, selector_mask, token_position, key_value_weight, key_value_bias, adapter_up_weight)
    group_size = Q_HEADS // KEY_VALUE_HEADS
    query_rot = rotate(queries.astype(jnp.float32).reshape(COMPLETION_COUNT, Q_HEADS, HEAD_WIDTH), token_position).astype(jnp.bfloat16)
    query_rot = query_rot.reshape(COMPLETION_COUNT, KEY_VALUE_HEADS, group_size, HEAD_WIDTH)

    def one_completion(item_args):
        query_one, parent_id, length, cache_rows, own_kv = item_args
        prefix_rows = lax.dynamic_index_in_dim(prefix_kv, parent_id, 0, keepdims=False).reshape(PREFIX_LENGTH, KEY_VALUE_HEADS, 2, HEAD_WIDTH)
        out_prefix, top_prefix, total_prefix = attend(query_one, prefix_rows[:, :, 0], prefix_rows[:, :, 1], jnp.ones((PREFIX_LENGTH,), dtype=bool))
        suffix_rows = jnp.concatenate([cache_rows.reshape(SUF, KEY_VALUE_HEADS, 2, HEAD_WIDTH), own_kv.reshape(1, KEY_VALUE_HEADS, 2, HEAD_WIDTH)], axis=0)
        valid_mask = jnp.concatenate([jnp.arange(SUF, dtype=jnp.int32) < length, jnp.ones((1,), dtype=bool)])
        out_suffix, top_suffix, total_suffix = attend(query_one, suffix_rows[:, :, 0], suffix_rows[:, :, 1], valid_mask)
        top_all = jnp.maximum(top_prefix, top_suffix)
        alpha_scale = jnp.exp(top_prefix - top_all)
        beta_scale = jnp.exp(top_suffix - top_all)
        merged = (alpha_scale[..., None] * out_prefix + beta_scale[..., None] * out_suffix) / (alpha_scale * total_prefix + beta_scale * total_suffix)[..., None]
        return merged.reshape(Q_HEADS * HEAD_WIDTH).astype(jnp.bfloat16)

    attn_out = lax.map(one_completion, (query_rot, parent, suffix_length_count, suffix_key_cache, latest_key_value))
    return prefix_kv, latest_key_value, attn_out
```

```python
import jax
import jax.numpy as jnp
import numpy as np
from jax import lax
from jax.experimental import pallas as pl
from jax.experimental.pallas import tpu as pltpu
from jax.sharding import PartitionSpec as P

HW = 128
RANK = 32
ROPE_BASE = 1000000.0
NEG = -1e30
CHUNKS = 3
BLK = 32
SROWS = 16
QMAX = 32766.0
MAGIC = 12582912.0
F32 = jnp.float32
BF16 = jnp.bfloat16


def rope_tables(first, count):
    half = HW // 2
    freq = (ROPE_BASE ** (-(np.arange(half, dtype=np.float64) * 2.0) / HW)).astype(np.float32)
    angle = np.arange(first, first + count, dtype=np.float32)[:, None] * freq[None, :]
    cosine = np.cos(angle.astype(np.float64)).astype(np.float32)
    sine = np.sin(angle.astype(np.float64)).astype(np.float32)
    return np.concatenate([cosine, cosine], 1), np.concatenate([-sine, sine], 1)


def three_parts(table):
    parts = []
    rest = table.astype(np.float32)
    for _ in range(3):
        part = rest.astype(BF16)
        parts.append(part)
        rest = rest - part.astype(np.float32)
    return parts


def turn(values, cosine, sine):
    return values * cosine + pltpu.roll(values, HW // 2, 1) * sine


def nn(a, b):
    return lax.dot_general(a, b, (((1,), (0,)), ((), ())), preferred_element_type=F32)


def nt(a, b):
    return lax.dot_general(a, b, (((1,), (1,)), ((), ())), preferred_element_type=F32)


def encode(values, out_ref, peak_ref):
    rows, cols = values.shape
    blocks = rows // BLK
    peak_ref[...] = jnp.full(peak_ref.shape, 1e-30, F32)
    for b in range(blocks):
        peak_ref[b : b + 1, :] = jnp.max(jnp.abs(values[b * BLK : (b + 1) * BLK]), axis=0, keepdims=True)
    level = jnp.ceil(jnp.log2(jnp.maximum(peak_ref[...], 1e-30)) * 256.0) + 1.0
    inverse = jnp.exp2(level * (-1.0 / 256.0)) * QMAX
    for b in range(blocks):
        scaled = values[b * BLK : (b + 1) * BLK] * inverse[b : b + 1, :]
        code = (scaled + MAGIC) - MAGIC
        out_ref[b * BLK : (b + 1) * BLK, :] = code.astype(jnp.int32).astype(jnp.int16)
    out_ref[rows : rows + SROWS, :] = level.astype(jnp.int32).astype(jnp.int16)


def scales(ref, rows):
    level = ref[rows : rows + SROWS, :].astype(jnp.int32).astype(F32)
    return jnp.exp2(level * (1.0 / 256.0)) * (1.0 / QMAX)


def decode(ref, scale, b):
    return ref[b * BLK : (b + 1) * BLK, :].astype(jnp.int32).astype(F32) * scale[b : b + 1, :]


def split_ranks(ranks, keep, is_key, key_ref, value_ref):
    width = ranks.shape[1]
    for mask, ref in ((keep & is_key, key_ref), (keep & jnp.logical_not(is_key), value_ref)):
        part = jnp.where(mask, ranks, 0.0)
        high = part.astype(BF16)
        ref[:, :width] = high
        ref[:, width:] = (part - high.astype(F32)).astype(BF16)


def project_body(with_latest, pf, *refs):
    if with_latest:
        (h, w, down, up, latest, parents, adapters, down_all, up_all,
         q1, q3, q2, own, xk, xv, codes, peaks, xlk, xlv, tile) = refs
    else:
        h, w, down, up, q1, q3, q2, own, xk, xv, codes, peaks, tile = refs
    g = pl.program_id(0)
    rows = h.shape[0]

    @pl.when(g == 0)
    def _():
        ranks = nn(h[...], down[...])
        lane = lax.broadcasted_iota(jnp.int32, ranks.shape, 1)
        split_ranks(ranks, (lane // (2 * RANK)) == pf[3], (lane % (2 * RANK)) < RANK, xk, xv)
        if with_latest:
            ranks = nn(latest[...], down_all[...])
            spot = lax.broadcasted_iota(jnp.int32, (parents.shape[0], adapters.shape[1]), 1)
            mine = jnp.sum(jnp.where(parents[...] == spot, adapters[...], 0), axis=1, keepdims=True)
            lane = lax.broadcasted_iota(jnp.int32, ranks.shape, 1)
            split_ranks(ranks, (lane // (2 * RANK)) == mine, (lane % (2 * RANK)) < RANK, xlk, xlv)

    base = nn(h[...], w[...])
    up2 = jnp.concatenate([up[...], up[...]], axis=0)
    tile[:rows, :HW] = base[:, :HW] + nn(xk[...], up2)
    tile[:rows, HW:] = base[:, HW:] + nn(xv[...], up2)
    if with_latest:
        base = nn(latest[...], w[...])
        up2 = jnp.concatenate([up_all[...], up_all[...]], axis=0)
        tile[rows:, :HW] = base[:, :HW] + nn(xlk[...], up2)
        tile[rows:, HW:] = base[:, HW:] + nn(xlv[...], up2)

    j = g // 2
    cols = pl.ds(pl.multiple_of((g % 2) * 2 * HW, 2 * HW), 2 * HW)

    @pl.when(j == 3)
    def _():
        own[:, cols] = tile[...]

    @pl.when(j < 3)
    def _():
        encode(tile[...], codes, peaks)
        for k, ref in enumerate((q1, q3, q2)):
            @pl.when(j == k)
            def _():
                ref[:, cols] = codes[...]


def project(chunk, rows, pf, hidden, weight, down, up, extra):
    with_latest = extra is not None
    depth = hidden.shape[1]
    total = rows + (extra[0].shape[0] if with_latest else 0)

    def column(g, pf):
        j = g // 2
        off = jnp.where(j == 0, 1, jnp.where(j == 1, 3, jnp.where(j == 2, 2, 0)))
        return ((pf[0] + off) % 4) * 2 + jnp.where(g % 2 == 0, pf[1], 1 - pf[1])

    in_specs = [
        pl.BlockSpec((rows, depth), lambda g, pf: (chunk, 0)),
        pl.BlockSpec((depth, 2 * HW), lambda g, pf: (0, column(g, pf))),
        pl.BlockSpec((depth, 4 * RANK), lambda g, pf: (0, pf[2])),
        pl.BlockSpec((4 * RANK, HW), lambda g, pf: (pf[2], column(g, pf))),
    ]
    args = [hidden, weight, down, up]
    scratch = [
        pltpu.VMEM((rows, 8 * RANK), BF16),
        pltpu.VMEM((rows, 8 * RANK), BF16),
        pltpu.VMEM((total + SROWS, 2 * HW), jnp.int16),
        pltpu.VMEM((SROWS, 2 * HW), F32),
    ]
    if with_latest:
        latest, parents, adapters = extra
        width = down.shape[1]
        in_specs += [
            pl.BlockSpec(latest.shape, lambda g, pf: (0, 0)),
            pl.BlockSpec(parents.shape, lambda g, pf: (0, 0)),
            pl.BlockSpec(adapters.shape, lambda g, pf: (0, 0)),
            pl.BlockSpec((depth, width), lambda g, pf: (0, 0)),
            pl.BlockSpec((width, HW), lambda g, pf: (0, column(g, pf))),
        ]
        args += [latest, parents, adapters, down, up]
        scratch += [pltpu.VMEM((latest.shape[0], 2 * width), BF16)] * 2
    scratch += [pltpu.VMEM((total, 2 * HW), F32)]
    fixed = lambda g, pf: (0, 0)
    code_shape = jax.ShapeDtypeStruct((total + SROWS, 4 * HW), jnp.int16)
    return pl.pallas_call(
        lambda pf, *refs: project_body(with_latest, pf, *refs),
        grid_spec=pltpu.PrefetchScalarGridSpec(
            num_scalar_prefetch=1,
            grid=(8,),
            in_specs=in_specs,
            out_specs=[pl.BlockSpec(code_shape.shape, fixed)] * 3 + [pl.BlockSpec((total, 4 * HW), fixed)],
            scratch_shapes=scratch,
        ),
        out_shape=[code_shape] * 3 + [jax.ShapeDtypeStruct((total, 4 * HW), F32)],
        compiler_params=pltpu.CompilerParams(vmem_limit_bytes=24 * 2**20),
        cost_estimate=pl.CostEstimate(
            flops=2 * total * depth * 16 * HW, bytes_accessed=depth * 32 * HW + total * depth * 2, transcendentals=0
        ),
        name="project",
    )(pf, *args)


def fold_body(a, b, c, own, out, keep, peaks, other):
    rows = own.shape[0]
    sa, sb, sc = scales(a, rows), scales(b, rows), scales(c, rows)
    for k in range(rows // BLK):
        span = slice(k * BLK, (k + 1) * BLK)
        total = own[span, :] + decode(a, sa, k) + decode(b, sb, k) + decode(c, sc, k)
        keep[span, :] = total[:, : 2 * HW]
        other[span, :] = total[:, 2 * HW :]
    encode(other[...], out, peaks)


def fold(a, b, c, own):
    rows = own.shape[0]
    return pl.pallas_call(
        fold_body,
        out_shape=[
            jax.ShapeDtypeStruct((rows + SROWS, 2 * HW), jnp.int16),
            jax.ShapeDtypeStruct((rows, 2 * HW), F32),
        ],
        scratch_shapes=[pltpu.VMEM((SROWS, 2 * HW), F32), pltpu.VMEM((rows, 2 * HW), F32)],
        compiler_params=pltpu.CompilerParams(vmem_limit_bytes=16 * 2**20),
        cost_estimate=pl.CostEstimate(flops=rows * 4 * HW * 8, bytes_accessed=rows * HW * 48, transcendentals=0),
        name="fold",
    )(a, b, c, own)


def dispatch_body(parents, lengths, queries, table, send, turned, cos_out, sin_out, place, counts, spread):
    comps = queries.shape[0]
    group = queries.shape[1] // HW
    spot = lax.broadcasted_iota(jnp.int32, (comps, table.shape[0]), 1)
    pick = (lengths[...] == spot + 1).astype(F32).astype(BF16)
    got = nn(pick, table[...])
    cosine = got[:, :HW] + got[:, HW : 2 * HW] + got[:, 2 * HW : 3 * HW]
    sine = got[:, 3 * HW : 4 * HW] + got[:, 4 * HW : 5 * HW] + got[:, 5 * HW :]
    cos_out[...] = cosine
    sin_out[...] = sine
    for h in range(group):
        part = queries[:, h * HW : (h + 1) * HW].astype(F32)
        turned[pl.ds(h, comps, stride=group), :] = turn(part, cosine, sine).astype(BF16).astype(F32)
    spread[...] = jnp.zeros(spread.shape, F32)

    def clear(i, carry):
        counts[i] = 0
        return carry

    lax.fori_loop(0, counts.shape[0], clear, 0)

    def put(c, carry):
        p = parents[c]
        s = counts[p]
        counts[p] = s + 1
        at = 2 * p + s
        place[c] = at
        to = pl.multiple_of(at * group, group)
        spread[pl.ds(to, group), :] = turned[pl.ds(pl.multiple_of(c * group, group), group), :]
        return carry

    lax.fori_loop(0, comps, put, 0)
    send[...] = spread[...].astype(BF16).reshape(send.shape)


def dispatch(parents, lengths, queries, table, prompts):
    comps = queries.shape[0]
    group = queries.shape[1] // HW
    vmem = pl.BlockSpec(memory_space=pltpu.VMEM)
    smem = pl.BlockSpec(memory_space=pltpu.SMEM)
    return pl.pallas_call(
        dispatch_body,
        in_specs=[smem, vmem, vmem, vmem],
        out_specs=[vmem, vmem, vmem, vmem, smem],
        out_shape=[
            jax.ShapeDtypeStruct((prompts, 2 * group, HW), BF16),
            jax.ShapeDtypeStruct((comps * group, HW), F32),
            jax.ShapeDtypeStruct((comps, HW), F32),
            jax.ShapeDtypeStruct((comps, HW), F32),
            jax.ShapeDtypeStruct((comps,), jnp.int32),
        ],
        scratch_shapes=[pltpu.SMEM((prompts,), jnp.int32), pltpu.VMEM((prompts * 2 * group, HW), F32)],
        compiler_params=pltpu.CompilerParams(vmem_limit_bytes=8 * 2**20),
        cost_estimate=pl.CostEstimate(flops=10**6, bytes_accessed=10**6, transcendentals=0),
        name="dispatch",
    )(parents, lengths, queries, table)


def suffix_body(turned, cache, came, keep, bias, cosine, sine, lengths, latest, out, stats, scores, weights, whole):
    comps = cosine.shape[0]
    first = keep.shape[0] - comps
    group = turned.shape[0] // comps
    scale = HW ** -0.5
    whole[...] = keep[first:, :] + bias[...] + decode(came, scales(came, keep.shape[0]), first // BLK)
    key = turn(whole[:, :HW], cosine[...], sine[...]).astype(BF16)
    value = whole[:, HW:].astype(BF16)
    latest[:, :HW] = key
    latest[:, HW:] = value

    def wide(rows):
        return jnp.broadcast_to(rows[:, None, :], (comps, group, HW)).reshape(comps * group, HW)

    for c in range(comps):
        span = slice(c * group, (c + 1) * group)
        scores[span, :] = nt(turned[span, :].astype(BF16), cache[c, :, :HW])
    own_score = jnp.sum(turned[...] * wide(key.astype(F32)), axis=1, keepdims=True) * scale
    slot = lax.broadcasted_iota(jnp.int32, scores.shape, 1)
    masked = jnp.where(slot < lengths[...], scores[...] * scale, NEG)
    top = jnp.maximum(jnp.max(masked, axis=1, keepdims=True), own_score)
    weight = jnp.exp(masked - top)
    own_weight = jnp.exp(own_score - top)
    total = jnp.sum(weight, axis=1, keepdims=True) + own_weight
    weights[...] = weight
    for c in range(comps):
        span = slice(c * group, (c + 1) * group)
        out[span, :] = nn(weights[span, :].astype(BF16), cache[c, :, HW:])
    out[...] = out[...] + own_weight.astype(BF16).astype(F32) * wide(value.astype(F32))
    stats[...] = jnp.where(slot < HW // 2, top, total)


def suffix(turned, cache, came, keep, bias, cosine, sine, lengths):
    comps = cosine.shape[0]
    rows = turned.shape[0]
    return pl.pallas_call(
        suffix_body,
        out_shape=[
            jax.ShapeDtypeStruct((comps, 2 * HW), BF16),
            jax.ShapeDtypeStruct((rows, HW), F32),
            jax.ShapeDtypeStruct((rows, HW), F32),
        ],
        scratch_shapes=[pltpu.VMEM((rows, HW), F32), pltpu.VMEM((rows, HW), F32), pltpu.VMEM((comps, 2 * HW), F32)],
        compiler_params=pltpu.CompilerParams(vmem_limit_bytes=16 * 2**20),
        cost_estimate=pl.CostEstimate(flops=10**7, bytes_accessed=10**7, transcendentals=0),
        name="suffix",
    )(turned, cache, came, keep, bias, cosine, sine, lengths)


def prefix_body(chunks, queries, bias, cosine, sine, *refs):
    came, keep = refs[:chunks], refs[chunks : 2 * chunks]
    kv, out = refs[2 * chunks :]
    length = kv.shape[0]
    rows = length // chunks
    for i in range(chunks):
        scale = scales(came[i], keep[i].shape[0])
        for k in range(rows // BLK):
            span = slice(i * rows + k * BLK, i * rows + (k + 1) * BLK)
            total = keep[i][k * BLK : (k + 1) * BLK, :] + decode(came[i], scale, k) + bias[...]
            kv[span, :HW] = turn(total[:, :HW], cosine[span, :], sine[span, :]).astype(BF16)
            kv[span, HW:] = total[:, HW:].astype(BF16)
    prompts, per, _ = queries.shape
    step = 8
    for s in range(0, prompts, step):
        q = queries[s : s + step].reshape(step * per, HW)
        scores = nt(q, kv[:, :HW]) * (HW ** -0.5)
        top = jnp.max(scores, axis=1, keepdims=True)
        weight = jnp.exp(scores - top)
        total = jnp.sum(weight, axis=1, keepdims=True)
        part = nn(weight.astype(BF16), kv[:, HW:])
        out[s : s + step, :per, :] = part.reshape(step, per, HW)
        lane = lax.broadcasted_iota(jnp.int32, (step * per, HW), 1)
        row = lax.broadcasted_iota(jnp.int32, (step * per, HW), 0) % per
        stat = jnp.where(lane == row, top, 0.0) + jnp.where(lane == row + per, total, 0.0)
        stat = jnp.sum(stat.reshape(step, per, HW), axis=1, keepdims=True)
        out[s : s + step, per:, :] = jnp.broadcast_to(stat, (step, 8, HW))


def prefix(queries, bias, cosine, sine, came, keep, length):
    chunks = len(came)
    prompts, per, _ = queries.shape
    return pl.pallas_call(
        lambda *refs: prefix_body(chunks, *refs),
        out_shape=[
            jax.ShapeDtypeStruct((length, 2 * HW), BF16),
            jax.ShapeDtypeStruct((prompts, per + 8, HW), F32),
        ],
        compiler_params=pltpu.CompilerParams(vmem_limit_bytes=24 * 2**20),
        cost_estimate=pl.CostEstimate(flops=2 * 10**8, bytes_accessed=10**7, transcendentals=10**6),
        name="prefix",
    )(queries, bias, cosine, sine, *came, *keep)


def merge_body(place, back, out, stats, attn, top_all, total_all, joined):
    prompts, per, _ = back.shape
    per -= 8
    rows = out.shape[0]
    comps = attn.shape[0]
    group = rows // comps
    lane = lax.broadcasted_iota(jnp.int32, (prompts * per, HW), 1)
    row = lax.broadcasted_iota(jnp.int32, (prompts * per, HW), 0) % per
    wide = jnp.broadcast_to(back[:, per : per + 1, :], (prompts, per, HW)).reshape(prompts * per, HW)
    top_all[...] = jnp.broadcast_to(
        jnp.sum(jnp.where(lane == row, wide, 0.0), axis=1, keepdims=True), top_all.shape)
    total_all[...] = jnp.broadcast_to(
        jnp.sum(jnp.where(lane == row + per, wide, 0.0), axis=1, keepdims=True), total_all.shape)

    for c in range(comps):
        at = place[c]
        src = pl.ds(pl.multiple_of(at * group, group), group)
        top_p, total_p = top_all[src, :], total_all[src, :]
        out_p = back[at // 2, pl.ds(pl.multiple_of((at % 2) * group, group), group), :]
        span = slice(c * group, (c + 1) * group)
        stat = stats[span, :]
        top_s, total_s = stat[:, :1], stat[:, HW // 2 : HW // 2 + 1]
        top = jnp.maximum(top_p, top_s)
        alpha = jnp.exp(top_p - top)
        beta = jnp.exp(top_s - top)
        joined[span, :] = (alpha * out_p + beta * out[span, :]) / (alpha * total_p + beta * total_s)
    for h in range(group):
        attn[:, h * HW : (h + 1) * HW] = joined[pl.ds(h, comps, stride=group), :].astype(BF16)


def merge(place, back, out, stats, comps):
    rows = out.shape[0]
    slots = back.shape[0] * (back.shape[1] - 8)
    vmem = pl.BlockSpec(memory_space=pltpu.VMEM)
    smem = pl.BlockSpec(memory_space=pltpu.SMEM)
    return pl.pallas_call(
        merge_body,
        in_specs=[smem, vmem, vmem, vmem],
        out_specs=vmem,
        out_shape=jax.ShapeDtypeStruct((comps, rows // comps * HW), BF16),
        scratch_shapes=[pltpu.VMEM((slots, HW), F32), pltpu.VMEM((slots, HW), F32), pltpu.VMEM((rows, HW), F32)],
        compiler_params=pltpu.CompilerParams(vmem_limit_bytes=8 * 2**20),
        cost_estimate=pl.CostEstimate(flops=10**6, bytes_accessed=10**6, transcendentals=10**5),
        name="merge",
    )(place, back, out, stats)


def on_device(
    prefix_hidden_states, latest_hidden, queries, suffix_key_cache, key_value_weight, key_value_bias,
    adapter_down_weight, adapter_up_weight, parents, adapter_index, suffix_length_count,
):
    rep = lax.axis_index("rep")
    tp = lax.axis_index("tp")
    y, z = tp // 2, tp % 2
    length = prefix_hidden_states.shape[1]
    comps = latest_hidden.shape[0]
    prompts = adapter_index.shape[0]
    group = queries.shape[1] // HW
    rows = length // CHUNKS
    along_y = lambda d: [(a * 2 + b, ((a + d) % 4) * 2 + b) for a in range(4) for b in range(2)]
    along_z = [(a * 2 + b, a * 2 + 1 - b) for a in range(4) for b in range(2)]

    adapter = lax.dynamic_index_in_dim(adapter_index, rep, 0, keepdims=False)
    pf = jnp.stack([y, z, adapter // 2, adapter % 2]).astype(jnp.int32)
    hidden = prefix_hidden_states[0]
    sent, own = [], []
    for i in range(CHUNKS):
        extra = (latest_hidden, parents, adapter_index.reshape(1, -1)) if i == 0 else None
        q1, q3, q2, mine = project(i, rows, pf, hidden, key_value_weight, adapter_down_weight, adapter_up_weight, extra)
        sent.append([
            lax.ppermute(q1, "tp", along_y(1)),
            lax.ppermute(q3, "tp", along_y(3)),
            lax.ppermute(q2, "tp", along_y(2)),
        ])
        own.append(mine)

    cos_t, sin_t = rope_tables(length + 1, suffix_key_cache.shape[1])
    table = jnp.asarray(np.concatenate(three_parts(cos_t) + three_parts(sin_t), 1))
    to_prompts, turned, cos_new, sin_new, place = dispatch(
        parents[:, 0], suffix_length_count.reshape(comps, 1), queries, table, prompts)
    here = lax.all_to_all(to_prompts, "rep", 0, 0, tiled=True)

    came, keep = [], []
    for i in range(CHUNKS):
        code, kept = fold(*sent[i], own[i])
        came.append(lax.ppermute(code, "tp", along_z))
        keep.append(kept)

    bias = key_value_bias.astype(F32).reshape(1, 2 * HW)
    latest_key_value, out_s, stats = suffix(
        turned, suffix_key_cache, came[0], keep[0], bias, cos_new, sin_new,
        jnp.repeat(suffix_length_count, group).reshape(comps * group, 1))
    cos_p, sin_p = rope_tables(0, length)
    prefix_kv, part = prefix(here, bias, jnp.asarray(cos_p), jnp.asarray(sin_p), came, keep, length)
    back = lax.all_to_all(part, "rep", 0, 0, tiled=True)
    attn_out = merge(place, back, out_s, stats, comps)
    return prefix_kv[None], latest_key_value, attn_out


def solution(mesh):
    in_specs = (
        P("rep", None, "tp"), P("rep", "tp"), P("rep", "tp"), P("rep", None, "tp"), P("tp", None), P("tp"),
        P("tp", None), P(), P("rep", None), P(), P("rep"),
    )
    out_specs = (P("rep", None, "tp"), P("rep", "tp"), P("rep", "tp"))
    return jax.shard_map(on_device, mesh=mesh, in_specs=in_specs, out_specs=out_specs, check_vma=False)
```

```python
import jax
import jax.numpy as jnp
import numpy as np
from jax import lax
from jax.experimental import pallas as pl
from jax.experimental.pallas import tpu as pltpu
from jax.sharding import PartitionSpec as P

HW = 128
RANK = 32
ROPE_BASE = 1000000.0
NEG = -1e30
PARTS = ((0, 384), (384, 384))
LIMIT = 52 * 2**20
BLK = 32
SROWS = 16
QMAX = 32766.0
MAGIC = 12582912.0
F32 = jnp.float32
BF16 = jnp.bfloat16


def rope_tables(first, count, step=1):
    half = HW // 2
    freq = (ROPE_BASE ** (-(np.arange(half, dtype=np.float64) * 2.0) / HW)).astype(np.float32)
    angle = np.arange(first, first + count, step, dtype=np.float32)[:, None] * freq[None, :]
    cosine = np.cos(angle.astype(np.float64)).astype(np.float32)
    sine = np.sin(angle.astype(np.float64)).astype(np.float32)
    return np.concatenate([cosine, cosine], 1), np.concatenate([-sine, sine], 1)


def turn(values, cosine, sine):
    return values * cosine + pltpu.roll(values, HW // 2, 1) * sine


def nn(a, b):
    return lax.dot_general(a, b, (((1,), (0,)), ((), ())), preferred_element_type=F32)


def nt(a, b):
    return lax.dot_general(a, b, (((1,), (1,)), ((), ())), preferred_element_type=F32)


def encode(values, out_ref, peak_ref):
    rows, cols = values.shape
    blocks = rows // BLK
    peak_ref[...] = jnp.full(peak_ref.shape, 1e-30, F32)
    for b in range(blocks):
        peak_ref[b : b + 1, :] = jnp.max(jnp.abs(values[b * BLK : (b + 1) * BLK]), axis=0, keepdims=True)
    level = jnp.ceil(jnp.log2(jnp.maximum(peak_ref[...], 1e-30)) * 256.0) + 1.0
    inverse = jnp.exp2(level * (-1.0 / 256.0)) * QMAX
    for b in range(blocks):
        scaled = values[b * BLK : (b + 1) * BLK] * inverse[b : b + 1, :]
        code = (scaled + MAGIC) - MAGIC
        out_ref[b * BLK : (b + 1) * BLK, :] = code.astype(jnp.int32).astype(jnp.int16)
    out_ref[rows : rows + SROWS, :] = level.astype(jnp.int32).astype(jnp.int16)


def scales(ref, rows):
    level = ref[rows : rows + SROWS, :].astype(jnp.int32).astype(F32)
    return jnp.exp2(level * (1.0 / 256.0)) * (1.0 / QMAX)


def decode(ref, scale, b):
    return ref[b * BLK : (b + 1) * BLK, :].astype(jnp.int32).astype(F32) * scale[b : b + 1, :]


def spread_up(up, span, heads, rows):
    key_row = (lax.broadcasted_iota(jnp.int32, (rows, HW), 0) % (2 * RANK)) < RANK
    zero = jnp.zeros((rows, HW), BF16)
    parts = []
    for head in heads:
        part = up[span, pl.ds(pl.multiple_of(head * HW, HW), HW)]
        parts += [jnp.where(key_row, part, zero), jnp.where(key_row, zero, part)]
    return jnp.concatenate(parts, axis=1)


def two_parts(values):
    high = values.astype(BF16)
    return high, (values - high.astype(F32)).astype(BF16)


class Loader:
    def __init__(self, adapter_of, hidden, weight, down, up, hx, wx, d, u, sems, whole):
        self.sems, self.hx, self.wx, self.d, self.u = sems, hx, wx, d, u
        self.depth = hidden.shape[1]
        tp = lax.axis_index("tp")
        self.y, self.z = tp // 2, tp % 2
        adapter = adapter_of[lax.axis_index("rep")]
        self.odd = adapter % 2
        spot = pl.ds(pl.multiple_of((adapter // 2) * (4 * RANK), 4 * RANK), 4 * RANK)
        self.pair = spot if whole else pl.ds(0, 4 * RANK)
        self.copies = [
            pltpu.make_async_copy(down if whole else down.at[:, spot], d, sems.at[0]),
            pltpu.make_async_copy(up if whole else up.at[spot, :], u, sems.at[1]),
        ]
        for first, rows in PARTS:
            span = pl.ds(first, rows)
            self.copies.append(
                pltpu.make_async_copy(hidden.at[span, :], hx.at[span, pl.ds(0, self.depth)], sems.at[len(self.copies)]))
        self.weight = weight

    def head(self, off, other):
        return ((self.y + off) % 4) * 2 + (1 - self.z if other else self.z)

    def weights(self, slot, off):
        made = []
        for other in range(2):
            at = pl.ds(pl.multiple_of(self.head(off, other) * (2 * HW), 2 * HW), 2 * HW)
            to = self.wx.at[slot, pl.ds(0, self.depth), pl.ds(other * 2 * HW, 2 * HW)]
            made.append(pltpu.make_async_copy(self.weight.at[:, at], to, self.sems.at[4 + 2 * slot + other]))
        return made

    def ranks(self, first, rows):
        span = slice(first, first + rows)
        got = nn(self.hx[span, : self.depth], self.d[:, self.pair])
        lane = lax.broadcasted_iota(jnp.int32, got.shape, 1)
        high, low = two_parts(jnp.where((lane // (2 * RANK)) == self.odd, got, 0.0))
        self.hx[span, self.depth : self.depth + 4 * RANK] = high
        self.hx[span, self.depth + 4 * RANK :] = low

    def extend(self, slot, off):
        ups = spread_up(self.u, self.pair, [self.head(off, 0), self.head(off, 1)], 4 * RANK)
        self.wx[slot, self.depth : self.depth + 4 * RANK, :] = ups
        self.wx[slot, self.depth + 4 * RANK :, :] = ups


def far_body(adapter_of, hidden, weight, down, up, out0, out1, hx, wx, d, u, tile, peaks, sems):
    load = Loader(adapter_of, hidden, weight, down, up, hx, wx, d, u, sems, False)
    blocks = load.weights(0, 2)
    for copy in load.copies[:3] + blocks + load.copies[3:]:
        copy.start()
    for copy in load.copies[:3]:
        copy.wait()
    load.ranks(*PARTS[0])
    load.extend(0, 2)
    for copy in blocks:
        copy.wait()
    for i, out in enumerate((out0, out1)):
        first, rows = PARTS[i]
        if i:
            load.copies[3].wait()
            load.ranks(first, rows)
        tile[...] = nn(hx[first : first + rows, :], wx[0])
        encode(tile[...], out, peaks)


def near_body(adapter_of, hidden, weight, down, up, latest, parents, adapters,
              direct0, direct1, near0, near1, own0, own1, last, hx, wx, d, u, tile, peaks, xl, sems):
    load = Loader(adapter_of, hidden, weight, down, up, hx, wx, d, u, sems, True)
    offs = (1, 3, 0, 2)
    blocks = [load.weights(k, off) for k, off in enumerate(offs)]
    for copy in load.copies + [copy for block in blocks for copy in block]:
        copy.start()
    for copy in load.copies:
        copy.wait()
    for part in PARTS:
        load.ranks(*part)
    ranks = nn(latest[...], d[...])
    names = lax.broadcasted_iota(jnp.int32, (parents.shape[0], adapters.shape[1]), 1)
    mine = jnp.sum(jnp.where(parents[...] == names, adapters[...], 0), axis=1, keepdims=True)
    lane = lax.broadcasted_iota(jnp.int32, ranks.shape, 1)
    high, low = two_parts(jnp.where((lane // (2 * RANK)) == mine, ranks, 0.0))
    xl[:, : ranks.shape[1]] = high
    xl[:, ranks.shape[1] :] = low
    first, rows = PARTS[1]

    def new_rows(k, off):
        ups = spread_up(u, slice(None), [load.head(off, 0), load.head(off, 1)], u.shape[0])
        return (nn(latest[...], wx[k, : load.depth, :]) + nn(xl[:, : ranks.shape[1]], ups)
                + nn(xl[:, ranks.shape[1] :], ups))

    for k, off in enumerate(offs):
        for copy in blocks[k]:
            copy.wait()
        if off == 2:
            encode(new_rows(k, off), last, peaks)
            continue
        load.extend(k, off)
        top = nn(hx[: PARTS[0][1], :], wx[k])
        if off == 3:
            tile[: PARTS[0][1], :] = top
            encode(tile[: PARTS[0][1], :], direct0, peaks)
        else:
            (near0 if off == 1 else own0)[...] = top
        to = {1: tile, 3: near1, 0: own1}[off]
        to[:rows, :] = nn(hx[first:, :], wx[k])
        to[rows:, :] = new_rows(k, off)
        if off == 1:
            encode(tile[...], direct1, peaks)


def project(adapter_index, hidden, weight, down, up, extra):
    depth = hidden.shape[1]
    news = extra[0].shape[0] if extra else 0
    length = hidden.shape[0]
    vmem = pl.BlockSpec(memory_space=pltpu.VMEM)
    hbm = pl.BlockSpec(memory_space=pltpu.HBM)
    smem = pl.BlockSpec(memory_space=pltpu.SMEM)
    code = lambda rows: jax.ShapeDtypeStruct((rows + SROWS, 4 * HW), jnp.int16)
    sums = lambda rows: jax.ShapeDtypeStruct((rows, 4 * HW), F32)
    r0, r1 = PARTS[0][1], PARTS[1][1] + news
    wide, tall, slots = (down.shape[1], up.shape[0], 4) if extra else (4 * RANK, 4 * RANK, 1)
    out_shape = [code(r0), code(r1), sums(r0), sums(r1), sums(r0), sums(r1), code(news)] if extra else [code(r0), code(r1)]
    scratch = [
        pltpu.VMEM((length, depth + 8 * RANK), BF16),
        pltpu.VMEM((slots, depth + 8 * RANK, 4 * HW), BF16),
        pltpu.VMEM((depth, wide), BF16),
        pltpu.VMEM((tall, up.shape[1]), BF16),
        pltpu.VMEM((r1, 4 * HW), F32),
        pltpu.VMEM((SROWS, 4 * HW), F32),
    ]
    if extra:
        scratch.append(pltpu.VMEM((news, 2 * wide), BF16))
    scratch.append(pltpu.SemaphoreType.DMA((4 + 2 * slots,)))
    return pl.pallas_call(
        near_body if extra else far_body,
        in_specs=[smem, hbm, hbm, hbm, hbm] + [vmem] * (3 if extra else 0),
        out_specs=[vmem] * len(out_shape),
        out_shape=out_shape,
        scratch_shapes=scratch,
        compiler_params=pltpu.CompilerParams(vmem_limit_bytes=LIMIT),
        cost_estimate=pl.CostEstimate(
            flops=2 * length * depth * (12 if extra else 4) * HW, bytes_accessed=8 * 10**6, transcendentals=0),
        name="project_near" if extra else "project_far",
    )(adapter_index, hidden, weight, down, up, *(extra or ()))


def relay_body(came, near, out, peaks, whole):
    sent = came.shape[0] - SROWS
    scale = scales(came, sent)
    for k in range(sent // BLK):
        span = slice(k * BLK, (k + 1) * BLK)
        whole[span, :] = near[span, :] + decode(came, scale, k)
    if sent < near.shape[0]:
        whole[sent:, :] = near[sent:, :]
    encode(whole[...], out, peaks)


def relay(came, near):
    rows, cols = near.shape
    return pl.pallas_call(
        relay_body,
        out_shape=jax.ShapeDtypeStruct((rows + SROWS, cols), jnp.int16),
        scratch_shapes=[pltpu.VMEM((SROWS, cols), F32), pltpu.VMEM((rows, cols), F32)],
        compiler_params=pltpu.CompilerParams(vmem_limit_bytes=LIMIT),
        cost_estimate=pl.CostEstimate(flops=rows * cols * 8, bytes_accessed=rows * cols * 8, transcendentals=0),
        name="relay",
    )(came, near)


def fold_body(a, b, own, *refs):
    last = refs[0] if len(refs) == 5 else None
    out, keep, peaks, other = refs[-4:]
    rows = own.shape[0]
    sa, sb = scales(a, rows), scales(b, rows)
    for k in range(rows // BLK):
        span = slice(k * BLK, (k + 1) * BLK)
        total = own[span, :] + decode(a, sa, k) + decode(b, sb, k)
        if last is not None and k == rows // BLK - 1:
            total = total + decode(last, scales(last, BLK), 0)
        keep[span, :] = total[:, : 2 * HW]
        other[span, :] = total[:, 2 * HW :]
    encode(other[...], out, peaks)


def fold(a, b, own, *last):
    rows = own.shape[0]
    return pl.pallas_call(
        fold_body,
        out_shape=[
            jax.ShapeDtypeStruct((rows + SROWS, 2 * HW), jnp.int16),
            jax.ShapeDtypeStruct((rows, 2 * HW), F32),
        ],
        scratch_shapes=[pltpu.VMEM((SROWS, 2 * HW), F32), pltpu.VMEM((rows, 2 * HW), F32)],
        compiler_params=pltpu.CompilerParams(vmem_limit_bytes=LIMIT),
        cost_estimate=pl.CostEstimate(flops=rows * 4 * HW * 8, bytes_accessed=rows * HW * 48, transcendentals=0),
        name="fold",
    )(a, b, own, *last)


def dispatch_body(parents, lengths, queries, table, send, turned, ropes, place, counts, spread):
    comps = queries.shape[0]
    group = queries.shape[1] // HW

    def look(c, carry):
        ropes[pl.ds(c, 1), :] = table[pl.ds(lengths[c] - 1, 1), :]
        return carry

    lax.fori_loop(0, comps, look, 0)
    for h in range(group):
        part = queries[:, h * HW : (h + 1) * HW].astype(F32)
        part = turn(part, ropes[:, :HW], ropes[:, HW:])
        turned[pl.ds(h, comps, stride=group), :] = part.astype(BF16).astype(F32)
    spread[...] = jnp.zeros(spread.shape, F32)

    def clear(i, carry):
        counts[i] = 0
        return carry

    lax.fori_loop(0, counts.shape[0], clear, 0)

    def put(c, carry):
        p = parents[c]
        s = counts[p]
        counts[p] = s + 1
        at = 2 * p + s
        place[c] = at
        to = pl.multiple_of(at * group, group)
        spread[pl.ds(to, group), :] = turned[pl.ds(pl.multiple_of(c * group, group), group), :]
        return carry

    lax.fori_loop(0, comps, put, 0)
    send[...] = spread[...].astype(BF16).reshape(send.shape)


def dispatch(parents, lengths, queries, table, prompts):
    comps = queries.shape[0]
    group = queries.shape[1] // HW
    vmem = pl.BlockSpec(memory_space=pltpu.VMEM)
    smem = pl.BlockSpec(memory_space=pltpu.SMEM)
    return pl.pallas_call(
        dispatch_body,
        in_specs=[smem, smem, vmem, vmem],
        out_specs=[vmem, vmem, vmem, smem],
        out_shape=[
            jax.ShapeDtypeStruct((prompts, 2 * group, HW), BF16),
            jax.ShapeDtypeStruct((comps * group, HW), F32),
            jax.ShapeDtypeStruct((comps, 2 * HW), F32),
            jax.ShapeDtypeStruct((comps,), jnp.int32),
        ],
        scratch_shapes=[pltpu.SMEM((prompts,), jnp.int32), pltpu.VMEM((prompts * 2 * group, HW), F32)],
        compiler_params=pltpu.CompilerParams(vmem_limit_bytes=LIMIT),
        cost_estimate=pl.CostEstimate(flops=10**6, bytes_accessed=10**6, transcendentals=0),
        name="dispatch",
    )(parents, lengths, queries, table)


def suffix_body(lengths, turned, cache, came, keep, bias, ropes, latest, out, stats, scores, weights, whole):
    comps = ropes.shape[0]
    first = keep.shape[0] - comps
    group = turned.shape[0] // comps
    scale = HW ** -0.5
    whole[...] = keep[first:, :] + bias[...] + decode(came, scales(came, keep.shape[0]), first // BLK)
    key = turn(whole[:, :HW], ropes[:, :HW], ropes[:, HW:]).astype(BF16)
    value = whole[:, HW:].astype(BF16)
    latest[:, :HW] = key
    latest[:, HW:] = value

    def wide(rows):
        return jnp.broadcast_to(rows[:, None, :], (comps, group, HW)).reshape(comps * group, HW)

    slot = lax.broadcasted_iota(jnp.int32, (group, HW), 1)
    for c in range(comps):
        span = slice(c * group, (c + 1) * group)
        score = nt(turned[span, :].astype(BF16), cache[c, :, :HW]) * scale
        scores[span, :] = jnp.where(slot < lengths[c], score, NEG)
    own_score = jnp.sum(turned[...] * wide(key.astype(F32)), axis=1, keepdims=True) * scale
    masked = scores[...]
    top = jnp.maximum(jnp.max(masked, axis=1, keepdims=True), own_score)
    weight = jnp.exp(masked - top)
    own_weight = jnp.exp(own_score - top)
    total = jnp.sum(weight, axis=1, keepdims=True) + own_weight
    weights[...] = weight
    for c in range(comps):
        span = slice(c * group, (c + 1) * group)
        out[span, :] = nn(weights[span, :].astype(BF16), cache[c, :, HW:])
    out[...] = out[...] + own_weight.astype(BF16).astype(F32) * wide(value.astype(F32))
    lane = lax.broadcasted_iota(jnp.int32, stats.shape, 1)
    stats[...] = jnp.where(lane < HW // 2, top, total)


def suffix(lengths, turned, cache, came, keep, bias, ropes):
    comps = ropes.shape[0]
    rows = turned.shape[0]
    vmem = pl.BlockSpec(memory_space=pltpu.VMEM)
    return pl.pallas_call(
        suffix_body,
        in_specs=[pl.BlockSpec(memory_space=pltpu.SMEM)] + [vmem] * 6,
        out_shape=[
            jax.ShapeDtypeStruct((comps, 2 * HW), BF16),
            jax.ShapeDtypeStruct((rows, HW), F32),
            jax.ShapeDtypeStruct((rows, HW), F32),
        ],
        scratch_shapes=[pltpu.VMEM((rows, HW), F32), pltpu.VMEM((rows, HW), F32), pltpu.VMEM((comps, 2 * HW), F32)],
        compiler_params=pltpu.CompilerParams(vmem_limit_bytes=LIMIT),
        cost_estimate=pl.CostEstimate(flops=10**7, bytes_accessed=10**7, transcendentals=0),
        name="suffix",
    )(lengths, turned, cache, came, keep, bias, ropes)


def prefix_body(queries, bias, turns, *refs):
    chunks = len(PARTS)
    came, keep = refs[:chunks], refs[chunks : 2 * chunks]
    kv, out = refs[2 * chunks :]
    blocks = kv.shape[0] // BLK
    cos_in, sin_in = turns[blocks:, :HW], turns[blocks:, HW:]
    for i, (first, rows) in enumerate(PARTS):
        scale = scales(came[i], keep[i].shape[0])
        for k in range(rows // BLK):
            span = slice(first + k * BLK, first + (k + 1) * BLK)
            total = keep[i][k * BLK : (k + 1) * BLK, :] + decode(came[i], scale, k) + bias[...]
            at = first // BLK + k
            cos_at, sin_at = turns[at : at + 1, :HW], turns[at : at + 1, HW:]
            cosine, sine = cos_at * cos_in - sin_at * sin_in, sin_at * cos_in + cos_at * sin_in
            kv[span, :HW] = turn(total[:, :HW], cosine, sine).astype(BF16)
            kv[span, HW:] = total[:, HW:].astype(BF16)
    prompts, per, _ = queries.shape
    step = 8
    for s in range(0, prompts, step):
        q = queries[s : s + step].reshape(step * per, HW)
        scores = nt(q, kv[:, :HW]) * (HW ** -0.5)
        top = jnp.max(scores, axis=1, keepdims=True)
        weight = jnp.exp(scores - top)
        total = jnp.sum(weight, axis=1, keepdims=True)
        part = nn(weight.astype(BF16), kv[:, HW:])
        out[s : s + step, :per, :] = part.reshape(step, per, HW)
        lane = lax.broadcasted_iota(jnp.int32, (step * per, HW), 1)
        row = lax.broadcasted_iota(jnp.int32, (step * per, HW), 0) % per
        stat = jnp.where(lane == row, top, 0.0) + jnp.where(lane == row + per, total, 0.0)
        stat = jnp.sum(stat.reshape(step, per, HW), axis=1, keepdims=True)
        out[s : s + step, per:, :] = jnp.broadcast_to(stat, (step, 8, HW))


def prefix(queries, bias, turns, came, keep, length):
    prompts, per, _ = queries.shape
    return pl.pallas_call(
        prefix_body,
        out_shape=[
            jax.ShapeDtypeStruct((length, 2 * HW), BF16),
            jax.ShapeDtypeStruct((prompts, per + 8, HW), F32),
        ],
        compiler_params=pltpu.CompilerParams(vmem_limit_bytes=LIMIT),
        cost_estimate=pl.CostEstimate(flops=2 * 10**8, bytes_accessed=10**7, transcendentals=10**6),
        name="prefix",
    )(queries, bias, turns, *came, *keep)


def merge_body(place, back, out, stats, attn, top_all, total_all, joined):
    prompts, per, _ = back.shape
    per -= 8
    rows = out.shape[0]
    comps = attn.shape[0]
    group = rows // comps
    lane = lax.broadcasted_iota(jnp.int32, (prompts * per, HW), 1)
    row = lax.broadcasted_iota(jnp.int32, (prompts * per, HW), 0) % per
    wide = jnp.broadcast_to(back[:, per : per + 1, :], (prompts, per, HW)).reshape(prompts * per, HW)
    top_all[...] = jnp.broadcast_to(
        jnp.sum(jnp.where(lane == row, wide, 0.0), axis=1, keepdims=True), top_all.shape)
    total_all[...] = jnp.broadcast_to(
        jnp.sum(jnp.where(lane == row + per, wide, 0.0), axis=1, keepdims=True), total_all.shape)

    for c in range(comps):
        at = place[c]
        src = pl.ds(pl.multiple_of(at * group, group), group)
        top_p, total_p = top_all[src, :], total_all[src, :]
        out_p = back[at // 2, pl.ds(pl.multiple_of((at % 2) * group, group), group), :]
        span = slice(c * group, (c + 1) * group)
        stat = stats[span, :]
        top_s, total_s = stat[:, :1], stat[:, HW // 2 : HW // 2 + 1]
        top = jnp.maximum(top_p, top_s)
        alpha = jnp.exp(top_p - top)
        beta = jnp.exp(top_s - top)
        joined[span, :] = (alpha * out_p + beta * out[span, :]) / (alpha * total_p + beta * total_s)
    for h in range(group):
        attn[:, h * HW : (h + 1) * HW] = joined[pl.ds(h, comps, stride=group), :].astype(BF16)


def merge(place, back, out, stats, comps):
    rows = out.shape[0]
    slots = back.shape[0] * (back.shape[1] - 8)
    vmem = pl.BlockSpec(memory_space=pltpu.VMEM)
    smem = pl.BlockSpec(memory_space=pltpu.SMEM)
    return pl.pallas_call(
        merge_body,
        in_specs=[smem, vmem, vmem, vmem],
        out_specs=vmem,
        out_shape=jax.ShapeDtypeStruct((comps, rows // comps * HW), BF16),
        scratch_shapes=[pltpu.VMEM((slots, HW), F32), pltpu.VMEM((slots, HW), F32), pltpu.VMEM((rows, HW), F32)],
        compiler_params=pltpu.CompilerParams(vmem_limit_bytes=LIMIT),
        cost_estimate=pl.CostEstimate(flops=10**6, bytes_accessed=10**6, transcendentals=10**5),
        name="merge",
    )(place, back, out, stats)


def on_device(
    prefix_hidden_states, latest_hidden, queries, suffix_key_cache, key_value_weight, key_value_bias,
    adapter_down_weight, adapter_up_weight, parents, adapter_index, suffix_length_count,
):
    length = prefix_hidden_states.shape[1]
    comps = latest_hidden.shape[0]
    prompts = adapter_index.shape[0]
    along_y = lambda d: [(a * 2 + b, ((a + d) % 4) * 2 + b) for a in range(4) for b in range(2)]
    along_z = [(a * 2 + b, a * 2 + 1 - b) for a in range(4) for b in range(2)]

    hidden = prefix_hidden_states[0]
    y_step = lambda value, d: lax.ppermute(value, "tp", along_y(d))
    weights = (key_value_weight, adapter_down_weight, adapter_up_weight)
    far0, far1 = project(adapter_index, hidden, *weights, None)
    far0, far1 = y_step(far0, 1), y_step(far1, -1)
    direct0, direct1, near0, near1, own0, own1, last = project(
        adapter_index, hidden, *weights, (latest_hidden, parents, adapter_index.reshape(1, -1)))
    direct0 = y_step(direct0, -1)
    joined0 = relay(far0, near0)
    joined0, direct1, last = lax.optimization_barrier((joined0, direct1, last))
    joined0 = y_step(joined0, 1)
    joined1 = relay(far1, near1)
    direct1, joined1, last = y_step(direct1, 1), y_step(joined1, -1), y_step(last, 2)

    cos_t, sin_t = rope_tables(length + 1, suffix_key_cache.shape[1])
    table = jnp.asarray(np.concatenate([cos_t, sin_t], 1))
    to_prompts, turned, ropes, place = dispatch(parents[:, 0], suffix_length_count, queries, table, prompts)
    here = lax.all_to_all(to_prompts, "rep", 0, 0, tiled=True)

    came, keep = [], []
    for args in ((joined0, direct0, own0), (joined1, direct1, own1, last)):
        code, kept = fold(*args)
        came.append(lax.ppermute(code, "tp", along_z))
        keep.append(kept)

    bias = key_value_bias.astype(F32).reshape(1, 2 * HW)
    latest_key_value, out_s, stats = suffix(
        suffix_length_count, turned, suffix_key_cache, came[1], keep[1], bias, ropes)
    blocks, within = rope_tables(0, length, BLK), rope_tables(0, BLK)
    turns = jnp.asarray(np.concatenate([np.concatenate(blocks, 1), np.concatenate(within, 1)], 0))
    prefix_kv, part = prefix(here, bias, turns, came, keep, length)
    back = lax.all_to_all(part, "rep", 0, 0, tiled=True)
    attn_out = merge(place, back, out_s, stats, comps)
    return prefix_kv[None], latest_key_value, attn_out


def solution(mesh):
    in_specs = (
        P("rep", None, "tp"), P("rep", "tp"), P("rep", "tp"), P("rep", None, "tp"), P("tp", None), P("tp"),
        P("tp", None), P(), P("rep", None), P(), P("rep"),
    )
    out_specs = (P("rep", None, "tp"), P("rep", "tp"), P("rep", "tp"))
    return jax.shard_map(on_device, mesh=mesh, in_specs=in_specs, out_specs=out_specs, check_vma=False)
```

```python
import jax
import jax.numpy as jnp
import numpy as np
from jax import lax
from jax.experimental import pallas as pl
from jax.experimental.pallas import tpu as pltpu
from jax.sharding import PartitionSpec as P

HW = 128
RANK = 32
ROPE_BASE = 1000000.0
NEG = -1e30
PARTS = ((0, 384), (384, 384))
LIMIT = 52 * 2**20
FAR_LIMIT = 54 * 2**20
NEAR_LIMIT = 52 * 2**20
BLK = 32
SROWS = 16
QMAX = 32766.0
MAGIC = 12582912.0
TOP_STEPS = (2.0**12, 2.0**-3, 2.0**-18)
TOTAL_STEPS = (2.0**-5, 2.0**-20)
F32 = jnp.float32
BF16 = jnp.bfloat16


def rope_tables(first, count, step=1):
    half = HW // 2
    freq = (ROPE_BASE ** (-(np.arange(half, dtype=np.float64) * 2.0) / HW)).astype(np.float32)
    angle = np.arange(first, first + count, step, dtype=np.float32)[:, None] * freq[None, :]
    cosine = np.cos(angle.astype(np.float64)).astype(np.float32)
    sine = np.sin(angle.astype(np.float64)).astype(np.float32)
    return np.concatenate([cosine, cosine], 1), np.concatenate([-sine, sine], 1)


def turn(values, cosine, sine):
    return values * cosine + pltpu.roll(values, HW // 2, 1) * sine


def nn(a, b):
    return lax.dot_general(a, b, (((1,), (0,)), ((), ())), preferred_element_type=F32)


def nt(a, b):
    return lax.dot_general(a, b, (((1,), (1,)), ((), ())), preferred_element_type=F32)


def near_int(values):
    return (values + MAGIC) - MAGIC


def encode(values, out_ref, peak_ref):
    rows, cols = values.shape
    blocks = rows // BLK
    peak_ref[...] = jnp.full(peak_ref.shape, 1e-30, F32)
    for b in range(blocks):
        peak_ref[b : b + 1, :] = jnp.max(jnp.abs(values[b * BLK : (b + 1) * BLK]), axis=0, keepdims=True)
    level = jnp.ceil(jnp.log2(jnp.maximum(peak_ref[...], 1e-30)) * 256.0) + 1.0
    inverse = jnp.exp2(level * (-1.0 / 256.0)) * QMAX
    for b in range(blocks):
        scaled = values[b * BLK : (b + 1) * BLK] * inverse[b : b + 1, :]
        code = near_int(scaled)
        out_ref[b * BLK : (b + 1) * BLK, :] = code.astype(jnp.int32).astype(jnp.int16)
    out_ref[rows : rows + SROWS, :] = level.astype(jnp.int32).astype(jnp.int16)


def scales(ref, rows):
    level = ref[rows : rows + SROWS, :].astype(jnp.int32).astype(F32)
    return jnp.exp2(level * (1.0 / 256.0)) * (1.0 / QMAX)


def decode(ref, scale, b):
    return ref[b * BLK : (b + 1) * BLK, :].astype(jnp.int32).astype(F32) * scale[b : b + 1, :]


def pieces(value, steps):
    got = []
    for step in steps:
        whole = near_int(value * (1.0 / step))
        value = value - whole * step
        got.append(whole)
    return got


def spread_up(up, span, rows):
    key_row = (lax.broadcasted_iota(jnp.int32, (rows, HW), 0) % (2 * RANK)) < RANK
    zero = jnp.zeros((rows, HW), BF16)
    parts = []
    for other in range(2):
        part = up[span, other * HW : (other + 1) * HW]
        parts += [jnp.where(key_row, part, zero), jnp.where(key_row, zero, part)]
    return jnp.concatenate(parts, axis=1)


def two_parts(values):
    high = values.astype(BF16)
    return high, (values - high.astype(F32)).astype(BF16)


def project_body(offs, places, adapter_of, parents, hidden, weight, down, up, latest, *refs):
    outs, (hx, wx, dp, d, u, tile, peaks, xl, mine, sems) = refs[:-10], refs[-10:]
    depth = hidden.shape[1]
    length, news = hidden.shape[0], latest.shape[0]
    (first0, rows0), (first1, rows1) = PARTS
    tp = lax.axis_index("tp")
    y, z = tp // 2, tp % 2
    adapter = adapter_of[lax.axis_index("rep")]
    pair = pl.ds(pl.multiple_of((adapter // 2) * (4 * RANK), 4 * RANK), 4 * RANK)

    def copy(src, dst, i):
        return pltpu.make_async_copy(src, dst, sems.at[i])

    blocks = []
    for k, off in enumerate(offs):
        made = []
        for other in range(2):
            head = ((y + off) % 4) * 2 + (1 - z if other else z)
            at = pl.ds(pl.multiple_of(head * (2 * HW), 2 * HW), 2 * HW)
            made.append(copy(weight.at[:, at], wx.at[k, pl.ds(0, depth), pl.ds(other * 2 * HW, 2 * HW)], 5 + 4 * k + other))
            at = pl.ds(pl.multiple_of(head * HW, HW), HW)
            made.append(copy(up.at[:, at], u.at[k, :, pl.ds(other * HW, HW)], 7 + 4 * k + other))
        blocks.append(made)
    early = [copy(down.at[:, pair], dp, 0), copy(hidden.at[pl.ds(first0, rows0), :], hx.at[pl.ds(first0, rows0), pl.ds(0, depth)], 1)]
    late = [
        copy(hidden.at[pl.ds(first1, rows1), :], hx.at[pl.ds(first1, rows1), pl.ds(0, depth)], 2),
        copy(latest, hx.at[pl.ds(length, news), pl.ds(0, depth)], 3),
        copy(down, d, 4),
    ]
    for c in early + blocks[0] + late + [c for made in blocks[1:] for c in made]:
        c.start()

    def name(c, carry):
        mine[pl.ds(c, 1), :] = jnp.full((1, HW), adapter_of[parents[c]], jnp.int32)
        return carry

    lax.fori_loop(0, news, name, 0)
    hx[length:, depth:] = jnp.zeros((news, 8 * RANK), BF16)

    def ranks(first, rows):
        span = slice(first, first + rows)
        got = nn(hx[span, :depth], dp[...])
        lane = lax.broadcasted_iota(jnp.int32, got.shape, 1)
        high, low = two_parts(jnp.where((lane // (2 * RANK)) == adapter % 2, got, 0.0))
        hx[span, depth : depth + 4 * RANK] = high
        hx[span, depth + 4 * RANK :] = low

    def part0(k):
        for c in blocks[k]:
            c.wait()
        ups = spread_up(u.at[k], pair, 4 * RANK)
        wx[k, depth : depth + 4 * RANK, :] = ups
        wx[k, depth + 4 * RANK :, :] = ups
        emit(0, offs[k], nn(hx[:rows0, :], wx[k]))

    def emit(part, off, values):
        ref, coded = places(outs, part, off)
        if coded:
            tile[: values.shape[0], :] = values
            encode(tile[: values.shape[0], :], ref, peaks)
        else:
            ref[...] = values

    for c in early:
        c.wait()
    ranks(first0, rows0)
    part0(0)
    for c in late:
        c.wait()
    ranks(first1, rows1)
    got = nn(hx[length:, :depth], d[...])
    lane = lax.broadcasted_iota(jnp.int32, got.shape, 1)
    high, low = two_parts(jnp.where((lane // (2 * RANK)) == mine[:, :1], got, 0.0))
    xl[:news, :] = high
    xl[news:, :] = low
    for k, off in enumerate(offs):
        if k:
            part0(k)
        added = nn(xl[...], spread_up(u.at[k], slice(None), up.shape[0]))
        ref, coded = places(outs, 1, off)
        to = tile if coded else ref
        to[...] = nn(hx[first1:, :], wx[k])
        to[rows1:, :] = to[rows1:, :] + (added[:news] + added[news:])
        if coded:
            encode(tile[...], ref, peaks)


def project_far(*args):
    return project((2,), lambda outs, part, off: (outs[part], True), 2, 0, *args)


def project_near(*args):
    table = {(0, 3): (0, True), (1, 1): (1, True), (0, 1): (2, False), (1, 3): (3, False), (0, 0): (4, False), (1, 0): (5, False)}

    def places(outs, part, off):
        at, coded = table[part, off]
        return outs[at], coded

    return project((3, 1, 0), places, 2, 4, *args)


def project(offs, places, codes, sums, limit, adapter_index, parents, hidden, weight, down, up, latest):
    depth = hidden.shape[1]
    length, news = hidden.shape[0], latest.shape[0]
    vmem = pl.BlockSpec(memory_space=pltpu.VMEM)
    hbm = pl.BlockSpec(memory_space=pltpu.HBM)
    smem = pl.BlockSpec(memory_space=pltpu.SMEM)
    rows = (PARTS[0][1], PARTS[1][1] + news)
    out_shape = [jax.ShapeDtypeStruct((rows[i % 2] + SROWS, 4 * HW), jnp.int16) for i in range(codes)]
    out_shape += [jax.ShapeDtypeStruct((rows[i % 2], 4 * HW), F32) for i in range(sums)]
    n = len(offs)
    return pl.pallas_call(
        lambda *refs: project_body(offs, places, *refs),
        in_specs=[smem, smem] + [hbm] * 5,
        out_specs=[vmem] * len(out_shape),
        out_shape=out_shape,
        scratch_shapes=[
            pltpu.VMEM((length + news, depth + 8 * RANK), BF16),
            pltpu.VMEM((n, depth + 8 * RANK, 4 * HW), BF16),
            pltpu.VMEM((depth, 4 * RANK), BF16),
            pltpu.VMEM(down.shape, BF16),
            pltpu.VMEM((n, up.shape[0], 2 * HW), BF16),
            pltpu.VMEM((rows[1], 4 * HW), F32),
            pltpu.VMEM((SROWS, 4 * HW), F32),
            pltpu.VMEM((2 * news, up.shape[0]), BF16),
            pltpu.VMEM((news, HW), jnp.int32),
            pltpu.SemaphoreType.DMA((5 + 4 * n,)),
        ],
        compiler_params=pltpu.CompilerParams(vmem_limit_bytes=limit),
        cost_estimate=pl.CostEstimate(
            flops=2 * length * depth * 4 * HW * n, bytes_accessed=2 * 10**6 * (n + 2), transcendentals=0),
        name="project%d" % n,
    )(adapter_index, parents, hidden, weight, down, up, latest)


def relay_body(came, near, out, peaks, whole):
    rows = near.shape[0]
    scale = scales(came, rows)
    for k in range(rows // BLK):
        span = slice(k * BLK, (k + 1) * BLK)
        whole[span, :] = near[span, :] + decode(came, scale, k)
    encode(whole[...], out, peaks)


def relay(came, near):
    rows, cols = near.shape
    return pl.pallas_call(
        relay_body,
        out_shape=jax.ShapeDtypeStruct((rows + SROWS, cols), jnp.int16),
        scratch_shapes=[pltpu.VMEM((SROWS, cols), F32), pltpu.VMEM((rows, cols), F32)],
        compiler_params=pltpu.CompilerParams(vmem_limit_bytes=LIMIT),
        cost_estimate=pl.CostEstimate(flops=rows * cols * 8, bytes_accessed=rows * cols * 8, transcendentals=0),
        name="relay",
    )(came, near)


def fold_body(a, b, own, out, keep, peaks, other):
    rows = own.shape[0]
    sa, sb = scales(a, rows), scales(b, rows)
    for k in range(rows // BLK):
        span = slice(k * BLK, (k + 1) * BLK)
        total = own[span, :] + decode(a, sa, k) + decode(b, sb, k)
        keep[span, :] = total[:, : 2 * HW]
        other[span, :] = total[:, 2 * HW :]
    encode(other[...], out, peaks)


def fold(a, b, own):
    rows = own.shape[0]
    return pl.pallas_call(
        fold_body,
        out_shape=[
            jax.ShapeDtypeStruct((rows + SROWS, 2 * HW), jnp.int16),
            jax.ShapeDtypeStruct((rows, 2 * HW), F32),
        ],
        scratch_shapes=[pltpu.VMEM((SROWS, 2 * HW), F32), pltpu.VMEM((rows, 2 * HW), F32)],
        compiler_params=pltpu.CompilerParams(vmem_limit_bytes=LIMIT),
        cost_estimate=pl.CostEstimate(flops=rows * 4 * HW * 8, bytes_accessed=rows * HW * 48, transcendentals=0),
        name="fold",
    )(a, b, own)


def dispatch_body(parents, lengths, queries, table, send, turned, ropes, place, counts, spread):
    comps = queries.shape[0]
    group = queries.shape[1] // HW

    def look(c, carry):
        ropes[pl.ds(c, 1), :] = table[pl.ds(lengths[c] - 1, 1), :]
        return carry

    lax.fori_loop(0, comps, look, 0)
    for h in range(group):
        part = queries[:, h * HW : (h + 1) * HW].astype(F32)
        part = turn(part, ropes[:, :HW], ropes[:, HW:])
        turned[pl.ds(h, comps, stride=group), :] = part.astype(BF16).astype(F32)
    spread[...] = jnp.zeros(spread.shape, F32)

    def clear(i, carry):
        counts[i] = 0
        return carry

    lax.fori_loop(0, counts.shape[0], clear, 0)

    def put(c, carry):
        p = parents[c]
        s = counts[p]
        counts[p] = s + 1
        at = 2 * p + s
        place[c] = at
        to = pl.multiple_of(at * group, group)
        spread[pl.ds(to, group), :] = turned[pl.ds(pl.multiple_of(c * group, group), group), :]
        return carry

    lax.fori_loop(0, comps, put, 0)
    send[...] = spread[...].astype(BF16).reshape(send.shape)


def dispatch(parents, lengths, queries, table, prompts):
    comps = queries.shape[0]
    group = queries.shape[1] // HW
    vmem = pl.BlockSpec(memory_space=pltpu.VMEM)
    smem = pl.BlockSpec(memory_space=pltpu.SMEM)
    return pl.pallas_call(
        dispatch_body,
        in_specs=[smem, smem, vmem, vmem],
        out_specs=[vmem, vmem, vmem, smem],
        out_shape=[
            jax.ShapeDtypeStruct((prompts, 2 * group, HW), BF16),
            jax.ShapeDtypeStruct((comps * group, HW), F32),
            jax.ShapeDtypeStruct((comps, 2 * HW), F32),
            jax.ShapeDtypeStruct((comps,), jnp.int32),
        ],
        scratch_shapes=[pltpu.SMEM((prompts,), jnp.int32), pltpu.VMEM((prompts * 2 * group, HW), F32)],
        compiler_params=pltpu.CompilerParams(vmem_limit_bytes=LIMIT),
        cost_estimate=pl.CostEstimate(flops=10**6, bytes_accessed=10**6, transcendentals=0),
        name="dispatch",
    )(parents, lengths, queries, table)


def suffix_body(lengths, turned, cache, came, keep, bias, ropes, latest, out, stats, scores, weights, whole):
    comps = ropes.shape[0]
    first = keep.shape[0] - comps
    group = turned.shape[0] // comps
    scale = HW ** -0.5
    whole[...] = keep[first:, :] + bias[...] + decode(came, scales(came, keep.shape[0]), first // BLK)
    key = turn(whole[:, :HW], ropes[:, :HW], ropes[:, HW:]).astype(BF16)
    value = whole[:, HW:].astype(BF16)
    latest[:, :HW] = key
    latest[:, HW:] = value

    def wide(rows):
        return jnp.broadcast_to(rows[:, None, :], (comps, group, HW)).reshape(comps * group, HW)

    slot = lax.broadcasted_iota(jnp.int32, (group, HW), 1)
    for c in range(comps):
        span = slice(c * group, (c + 1) * group)
        score = nt(turned[span, :].astype(BF16), cache[c, :, :HW]) * scale
        scores[span, :] = jnp.where(slot < lengths[c], score, NEG)
    own_score = jnp.sum(turned[...] * wide(key.astype(F32)), axis=1, keepdims=True) * scale
    masked = scores[...]
    top = jnp.maximum(jnp.max(masked, axis=1, keepdims=True), own_score)
    weight = jnp.exp(masked - top)
    own_weight = jnp.exp(own_score - top)
    total = jnp.sum(weight, axis=1, keepdims=True) + own_weight
    weights[...] = weight
    for c in range(comps):
        span = slice(c * group, (c + 1) * group)
        out[span, :] = nn(weights[span, :].astype(BF16), cache[c, :, HW:])
    out[...] = out[...] + own_weight.astype(BF16).astype(F32) * wide(value.astype(F32))
    lane = lax.broadcasted_iota(jnp.int32, stats.shape, 1)
    stats[...] = jnp.where(lane < HW // 2, top, total)


def suffix(lengths, turned, cache, came, keep, bias, ropes):
    comps = ropes.shape[0]
    rows = turned.shape[0]
    vmem = pl.BlockSpec(memory_space=pltpu.VMEM)
    return pl.pallas_call(
        suffix_body,
        in_specs=[pl.BlockSpec(memory_space=pltpu.SMEM)] + [vmem] * 6,
        out_shape=[
            jax.ShapeDtypeStruct((comps, 2 * HW), BF16),
            jax.ShapeDtypeStruct((rows, HW), F32),
            jax.ShapeDtypeStruct((rows, HW), F32),
        ],
        scratch_shapes=[pltpu.VMEM((rows, HW), F32), pltpu.VMEM((rows, HW), F32), pltpu.VMEM((comps, 2 * HW), F32)],
        compiler_params=pltpu.CompilerParams(vmem_limit_bytes=LIMIT),
        cost_estimate=pl.CostEstimate(flops=10**7, bytes_accessed=10**7, transcendentals=0),
        name="suffix",
    )(lengths, turned, cache, came, keep, bias, ropes)


def prefix_body(queries, bias, turns, *refs):
    chunks = len(PARTS)
    came, keep = refs[:chunks], refs[chunks : 2 * chunks]
    kv, out = refs[2 * chunks :]
    blocks = kv.shape[0] // BLK
    cos_in, sin_in = turns[blocks:, :HW], turns[blocks:, HW:]
    for i, (first, rows) in enumerate(PARTS):
        scale = scales(came[i], keep[i].shape[0])
        for k in range(rows // BLK):
            span = slice(first + k * BLK, first + (k + 1) * BLK)
            total = keep[i][k * BLK : (k + 1) * BLK, :] + decode(came[i], scale, k) + bias[...]
            at = first // BLK + k
            cos_at, sin_at = turns[at : at + 1, :HW], turns[at : at + 1, HW:]
            cosine, sine = cos_at * cos_in - sin_at * sin_in, sin_at * cos_in + cos_at * sin_in
            kv[span, :HW] = turn(total[:, :HW], cosine, sine).astype(BF16)
            kv[span, HW:] = total[:, HW:].astype(BF16)
    prompts, per, _ = queries.shape
    step = 8
    for s in range(0, prompts, step):
        q = queries[s : s + step].reshape(step * per, HW)
        scores = nt(q, kv[:, :HW]) * (HW ** -0.5)
        top = jnp.max(scores, axis=1, keepdims=True)
        weight = jnp.exp(scores - top)
        total = jnp.sum(weight, axis=1, keepdims=True)
        part = nn(weight.astype(BF16), kv[:, HW:])
        peak = jnp.maximum(jnp.max(jnp.abs(part), axis=1, keepdims=True), 1e-30)
        level = jnp.ceil(jnp.log2(peak) * 256.0) + 1.0
        code = near_int(part * (jnp.exp2(level * (-1.0 / 256.0)) * QMAX))
        lane = lax.broadcasted_iota(jnp.int32, (step * per, HW), 1)
        row = lax.broadcasted_iota(jnp.int32, (step * per, HW), 0) % per
        stat = jnp.zeros((step * per, HW), F32)
        for i, piece in enumerate(pieces(top, TOP_STEPS) + pieces(total, TOTAL_STEPS) + [level]):
            stat = stat + jnp.where(lane == row + i * per, piece, 0.0)
        stat = jnp.sum(stat.reshape(step, per, HW), axis=1, keepdims=True)
        whole = jnp.concatenate([code.reshape(step, per, HW), jnp.broadcast_to(stat, (step, 8, HW))], axis=1)
        out[s : s + step] = whole.astype(jnp.int32).astype(jnp.int16)


def prefix(queries, bias, turns, came, keep, length):
    prompts, per, _ = queries.shape
    return pl.pallas_call(
        prefix_body,
        out_shape=[
            jax.ShapeDtypeStruct((length, 2 * HW), BF16),
            jax.ShapeDtypeStruct((prompts, per + 8, HW), jnp.int16),
        ],
        compiler_params=pltpu.CompilerParams(vmem_limit_bytes=LIMIT),
        cost_estimate=pl.CostEstimate(flops=2 * 10**8, bytes_accessed=10**7, transcendentals=10**6),
        name="prefix",
    )(queries, bias, turns, *came, *keep)


def merge_body(place, back, out, stats, attn, spread, side, joined):
    prompts, per, _ = back.shape
    per -= 8
    rows = out.shape[0]
    comps = attn.shape[0]
    group = rows // comps
    came = back[...].astype(jnp.int32).astype(F32)
    spread[...] = came
    for c in range(comps):
        at = place[c]
        span = slice(c * group, (c + 1) * group)
        slot = at % 2
        joined[span, :] = spread[at // 2, pl.ds(pl.multiple_of(slot * group, group), group), :]
        side[span, :] = jnp.where(
            lax.broadcasted_iota(jnp.int32, (group, HW), 1) % per
            == lax.broadcasted_iota(jnp.int32, (group, HW), 0) + slot * group,
            spread[at // 2, per:, :], 0.0)
    lane = lax.broadcasted_iota(jnp.int32, (rows, HW), 1)
    stat = []
    for i in range(len(TOP_STEPS) + len(TOTAL_STEPS) + 1):
        stat.append(jnp.sum(jnp.where(lane // per == i, side[...], 0.0), axis=1, keepdims=True))
    top_p = sum(piece * step for piece, step in zip(stat, TOP_STEPS))
    total_p = sum(piece * step for piece, step in zip(stat[len(TOP_STEPS) :], TOTAL_STEPS))
    out_p = joined[...] * (jnp.exp2(stat[-1] * (1.0 / 256.0)) * (1.0 / QMAX))
    top_s, total_s = stats[:, :1], stats[:, HW // 2 : HW // 2 + 1]
    top = jnp.maximum(top_p, top_s)
    alpha = jnp.exp(top_p - top)
    beta = jnp.exp(top_s - top)
    joined[...] = (alpha * out_p + beta * out[...]) / (alpha * total_p + beta * total_s)
    for h in range(group):
        attn[:, h * HW : (h + 1) * HW] = joined[pl.ds(h, comps, stride=group), :].astype(BF16)


def merge(place, back, out, stats, comps):
    rows = out.shape[0]
    vmem = pl.BlockSpec(memory_space=pltpu.VMEM)
    smem = pl.BlockSpec(memory_space=pltpu.SMEM)
    return pl.pallas_call(
        merge_body,
        in_specs=[smem, vmem, vmem, vmem],
        out_specs=vmem,
        out_shape=jax.ShapeDtypeStruct((comps, rows // comps * HW), BF16),
        scratch_shapes=[pltpu.VMEM(back.shape, F32), pltpu.VMEM((rows, HW), F32), pltpu.VMEM((rows, HW), F32)],
        compiler_params=pltpu.CompilerParams(vmem_limit_bytes=LIMIT),
        cost_estimate=pl.CostEstimate(flops=10**6, bytes_accessed=10**6, transcendentals=10**5),
        name="merge",
    )(place, back, out, stats)


def on_device(
    prefix_hidden_states, latest_hidden, queries, suffix_key_cache, key_value_weight, key_value_bias,
    adapter_down_weight, adapter_up_weight, parents, adapter_index, suffix_length_count,
):
    length = prefix_hidden_states.shape[1]
    comps = latest_hidden.shape[0]
    prompts = adapter_index.shape[0]
    along_y = lambda d: [(a * 2 + b, ((a + d) % 4) * 2 + b) for a in range(4) for b in range(2)]
    along_z = [(a * 2 + b, a * 2 + 1 - b) for a in range(4) for b in range(2)]

    hidden = prefix_hidden_states[0]
    y_step = lambda value, d: lax.ppermute(value, "tp", along_y(d))
    parent = parents[:, 0]
    inputs = (adapter_index, parent, hidden, key_value_weight, adapter_down_weight, adapter_up_weight, latest_hidden)
    far0, far1 = project_far(FAR_LIMIT, *inputs)
    far0, far1 = y_step(far0, 1), y_step(far1, -1)
    direct0, direct1, near0, near1, own0, own1 = project_near(NEAR_LIMIT, *inputs)
    direct0 = y_step(direct0, -1)
    joined0 = relay(far0, near0)
    joined0, queries, far1 = lax.optimization_barrier((joined0, queries, far1))
    joined0 = y_step(joined0, 1)
    joined1 = relay(far1, near1)

    cos_t, sin_t = rope_tables(length + 1, suffix_key_cache.shape[1])
    table = jnp.asarray(np.concatenate([cos_t, sin_t], 1))
    to_prompts, turned, ropes, place = dispatch(parent, suffix_length_count, queries, table, prompts)
    here = lax.all_to_all(to_prompts, "rep", 0, 0, tiled=True)
    joined1, direct1, to_prompts = lax.optimization_barrier((joined1, direct1, to_prompts))
    direct1, joined1 = y_step(direct1, 1), y_step(joined1, -1)
    joined0, direct0, here = lax.optimization_barrier((joined0, direct0, here))
    code0, keep0 = fold(joined0, direct0, own0)
    came0 = lax.ppermute(code0, "tp", along_z)
    code1, keep1 = fold(joined1, direct1, own1)
    came1 = lax.ppermute(code1, "tp", along_z)
    came, keep = (came0, came1), (keep0, keep1)

    bias = key_value_bias.astype(F32).reshape(1, 2 * HW)
    latest_key_value, out_s, stats = suffix(
        suffix_length_count, turned, suffix_key_cache, came[1], keep[1], bias, ropes)
    blocks, within = rope_tables(0, length, BLK), rope_tables(0, BLK)
    turns = jnp.asarray(np.concatenate([np.concatenate(blocks, 1), np.concatenate(within, 1)], 0))
    prefix_kv, part = prefix(here, bias, turns, came, keep, length)
    back = lax.all_to_all(part, "rep", 0, 0, tiled=True)
    attn_out = merge(place, back, out_s, stats, comps)
    return prefix_kv[None], latest_key_value, attn_out


def solution(mesh):
    in_specs = (
        P("rep", None, "tp"), P("rep", "tp"), P("rep", "tp"), P("rep", None, "tp"), P("tp", None), P("tp"),
        P("tp", None), P(), P("rep", None), P(), P("rep"),
    )
    out_specs = (P("rep", None, "tp"), P("rep", "tp"), P("rep", "tp"))
    return jax.shard_map(on_device, mesh=mesh, in_specs=in_specs, out_specs=out_specs, check_vma=False)
```

```python
import jax
import jax.numpy as jnp
import numpy as np
from jax import lax
from jax.experimental import pallas as pl
from jax.experimental.pallas import tpu as pltpu
from jax.sharding import PartitionSpec as P

HW = 128
RANK = 32
ROPE_BASE = 1000000.0
NEG = -1e30
PARTS = ((0, 384), (384, 384))
LIMIT = 16 * 2**20
FAR_LIMIT = 16 * 2**20
NEAR_LIMIT = 20 * 2**20
BLK = 32
SROWS = 16
QMAX = 32766.0
MAGIC = 12582912.0
TOP_STEPS = (2.0**12, 2.0**-3, 2.0**-18)
TOTAL_STEPS = (2.0**-5, 2.0**-20)
F32 = jnp.float32
BF16 = jnp.bfloat16


def rope_tables(first, count, step=1):
    half = HW // 2
    freq = (ROPE_BASE ** (-(np.arange(half, dtype=np.float64) * 2.0) / HW)).astype(np.float32)
    angle = np.arange(first, first + count, step, dtype=np.float32)[:, None] * freq[None, :]
    cosine = np.cos(angle.astype(np.float64)).astype(np.float32)
    sine = np.sin(angle.astype(np.float64)).astype(np.float32)
    return np.concatenate([cosine, cosine], 1), np.concatenate([-sine, sine], 1)


def turn(values, cosine, sine):
    return values * cosine + pltpu.roll(values, HW // 2, 1) * sine


def nn(a, b):
    return lax.dot_general(a, b, (((1,), (0,)), ((), ())), preferred_element_type=F32)


def nt(a, b):
    return lax.dot_general(a, b, (((1,), (1,)), ((), ())), preferred_element_type=F32)


def near_int(values):
    return (values + MAGIC) - MAGIC


def encode(values, out_ref, peak_ref):
    rows, cols = values.shape
    blocks = rows // BLK
    peak_ref[...] = jnp.full(peak_ref.shape, 1e-30, F32)
    for b in range(blocks):
        peak_ref[b : b + 1, :] = jnp.max(jnp.abs(values[b * BLK : (b + 1) * BLK]), axis=0, keepdims=True)
    level = jnp.ceil(jnp.log2(jnp.maximum(peak_ref[...], 1e-30)) * 256.0) + 1.0
    inverse = jnp.exp2(level * (-1.0 / 256.0)) * QMAX
    for b in range(blocks):
        scaled = values[b * BLK : (b + 1) * BLK] * inverse[b : b + 1, :]
        code = near_int(scaled)
        out_ref[b * BLK : (b + 1) * BLK, :] = code.astype(jnp.int32).astype(jnp.int16)
    out_ref[rows : rows + SROWS, :] = level.astype(jnp.int32).astype(jnp.int16)


def scales(ref, rows):
    level = ref[rows : rows + SROWS, :].astype(jnp.int32).astype(F32)
    return jnp.exp2(level * (1.0 / 256.0)) * (1.0 / QMAX)


def decode(ref, scale, b):
    return ref[b * BLK : (b + 1) * BLK, :].astype(jnp.int32).astype(F32) * scale[b : b + 1, :]


def pieces(value, steps):
    got = []
    for step in steps:
        whole = near_int(value * (1.0 / step))
        value = value - whole * step
        got.append(whole)
    return got


def spread_up(up, span, rows):
    key_row = (lax.broadcasted_iota(jnp.int32, (rows, HW), 0) % (2 * RANK)) < RANK
    zero = jnp.zeros((rows, HW), BF16)
    parts = []
    for other in range(2):
        part = up[span, other * HW : (other + 1) * HW]
        parts += [jnp.where(key_row, part, zero), jnp.where(key_row, zero, part)]
    return jnp.concatenate(parts, axis=1)


def two_parts(values):
    high = values.astype(BF16)
    return high, (values - high.astype(F32)).astype(BF16)


def project_body(offs, places, known, adapter_of, parents, hidden, weight, down, up, latest, *refs):
    if known:
        (xr_in, xl), refs = refs[:2], refs[2:]
        outs, (hx, wx, u, tile, peaks, sems) = refs[:-6], refs[-6:]
    else:
        outs, (xr_out, xl), (hx, wx, u, tile, peaks, dp, d, mine, sems) = refs[:-11], refs[-11:-9], refs[-9:]
    depth = hidden.shape[1]
    length, news = hidden.shape[0], latest.shape[0]
    (first0, rows0), (first1, rows1) = PARTS
    tp = lax.axis_index("tp")
    y, z = tp // 2, tp % 2
    adapter = adapter_of[lax.axis_index("rep")]
    pair = pl.ds(pl.multiple_of((adapter // 2) * (4 * RANK), 4 * RANK), 4 * RANK)

    def copy(src, dst, i):
        return pltpu.make_async_copy(src, dst, sems.at[i])

    blocks = []
    for k, off in enumerate(offs):
        made = []
        for other in range(2):
            head = ((y + off) % 4) * 2 + (1 - z if other else z)
            at = pl.ds(pl.multiple_of(head * (2 * HW), 2 * HW), 2 * HW)
            made.append(copy(weight.at[:, at], wx.at[k, pl.ds(0, depth), pl.ds(other * 2 * HW, 2 * HW)], 5 + 4 * k + other))
            at = pl.ds(pl.multiple_of(head * HW, HW), HW)
            made.append(copy(up.at[:, at], u.at[k, :, pl.ds(other * HW, HW)], 7 + 4 * k + other))
        blocks.append(made)
    early = [copy(hidden.at[pl.ds(first0, rows0), :], hx.at[pl.ds(first0, rows0), pl.ds(0, depth)], 1)]
    late = [
        copy(hidden.at[pl.ds(first1, rows1), :], hx.at[pl.ds(first1, rows1), pl.ds(0, depth)], 2),
        copy(latest, hx.at[pl.ds(length, news), pl.ds(0, depth)], 3),
    ]
    if known:
        hx[:, depth:] = xr_in[...]
    else:
        early.insert(0, copy(down.at[:, pair], dp, 0))
        late.append(copy(down, d, 4))
    for c in early + blocks[0] + late + [c for made in blocks[1:] for c in made]:
        c.start()

    if not known:
        def name(c, carry):
            mine[pl.ds(c, 1), :] = jnp.full((1, HW), adapter_of[parents[c]], jnp.int32)
            return carry

        lax.fori_loop(0, news, name, 0)
        hx[length:, depth:] = jnp.zeros((news, 8 * RANK), BF16)

    def ranks(first, rows):
        span = slice(first, first + rows)
        got = nn(hx[span, :depth], dp[...])
        lane = lax.broadcasted_iota(jnp.int32, got.shape, 1)
        high, low = two_parts(jnp.where((lane // (2 * RANK)) == adapter % 2, got, 0.0))
        hx[span, depth : depth + 4 * RANK] = high
        hx[span, depth + 4 * RANK :] = low

    def part0(k):
        for c in blocks[k]:
            c.wait()
        ups = spread_up(u.at[k], pair, 4 * RANK)
        wx[k, depth : depth + 4 * RANK, :] = ups
        wx[k, depth + 4 * RANK :, :] = ups
        emit(0, offs[k], nn(hx[:rows0, :], wx[k]))

    def emit(part, off, values):
        ref, coded = places(outs, part, off)
        if coded:
            tile[: values.shape[0], :] = values
            encode(tile[: values.shape[0], :], ref, peaks)
        else:
            ref[...] = values

    for c in early:
        c.wait()
    if not known:
        ranks(first0, rows0)
    part0(0)
    for c in late:
        c.wait()
    if not known:
        ranks(first1, rows1)
        got = nn(hx[length:, :depth], d[...])
        lane = lax.broadcasted_iota(jnp.int32, got.shape, 1)
        high, low = two_parts(jnp.where((lane // (2 * RANK)) == mine[:, :1], got, 0.0))
        xl[:news, :] = high
        xl[news:, :] = low
        xr_out[...] = hx[:, depth:]
    for k, off in enumerate(offs):
        if k:
            part0(k)
        added = nn(xl[...], spread_up(u.at[k], slice(None), up.shape[0]))
        ref, coded = places(outs, 1, off)
        to = tile if coded else ref
        to[...] = nn(hx[first1:, :], wx[k])
        to[rows1:, :] = to[rows1:, :] + (added[:news] + added[news:])
        if coded:
            encode(tile[...], ref, peaks)


def project_far(*args):
    return project((2,), lambda outs, part, off: (outs[part], True), 2, 0, *args, ())


def project_near(*args):
    table = {(0, 3): (0, True), (1, 1): (1, True), (0, 1): (2, False), (1, 3): (3, False), (0, 0): (4, False), (1, 0): (5, False)}

    def places(outs, part, off):
        at, coded = table[part, off]
        return outs[at], coded

    return project((3, 1, 0), places, 2, 4, *args)


def project(offs, places, codes, sums, limit, adapter_index, parents, hidden, weight, down, up, latest, known):
    depth = hidden.shape[1]
    length, news = hidden.shape[0], latest.shape[0]
    vmem = pl.BlockSpec(memory_space=pltpu.VMEM)
    hbm = pl.BlockSpec(memory_space=pltpu.HBM)
    smem = pl.BlockSpec(memory_space=pltpu.SMEM)
    rows = (PARTS[0][1], PARTS[1][1] + news)
    out_shape = [jax.ShapeDtypeStruct((rows[i % 2] + SROWS, 4 * HW), jnp.int16) for i in range(codes)]
    out_shape += [jax.ShapeDtypeStruct((rows[i % 2], 4 * HW), F32) for i in range(sums)]
    n = len(offs)
    ranks = [
        jax.ShapeDtypeStruct((length + news, 8 * RANK), BF16),
        jax.ShapeDtypeStruct((2 * news, up.shape[0]), BF16),
    ]
    if known:
        own = []
    else:
        out_shape += ranks
        own = [pltpu.VMEM((depth, 4 * RANK), BF16), pltpu.VMEM(down.shape, BF16), pltpu.VMEM((news, HW), jnp.int32)]
    return pl.pallas_call(
        lambda *refs: project_body(offs, places, bool(known), *refs),
        in_specs=[smem, smem] + [hbm] * 5 + [vmem] * len(known),
        out_specs=[vmem] * len(out_shape),
        out_shape=out_shape,
        scratch_shapes=[
            pltpu.VMEM((length + news, depth + 8 * RANK), BF16),
            pltpu.VMEM((n, depth + 8 * RANK, 4 * HW), BF16),
            pltpu.VMEM((n, up.shape[0], 2 * HW), BF16),
            pltpu.VMEM((rows[1], 4 * HW), F32),
            pltpu.VMEM((SROWS, 4 * HW), F32),
            *own,
            pltpu.SemaphoreType.DMA((5 + 4 * n,)),
        ],
        compiler_params=pltpu.CompilerParams(vmem_limit_bytes=limit),
        cost_estimate=pl.CostEstimate(
            flops=2 * length * depth * 4 * HW * n, bytes_accessed=2 * 10**6 * (n + 2), transcendentals=0),
        name="project%d" % n,
    )(adapter_index, parents, hidden, weight, down, up, latest, *known)


def relay_body(came0, near0, came1, near1, out0, out1, peaks, whole):
    for came, near, out in ((came0, near0, out0), (came1, near1, out1)):
        rows = near.shape[0]
        scale = scales(came, rows)
        for k in range(rows // BLK):
            span = slice(k * BLK, (k + 1) * BLK)
            whole[span, :] = near[span, :] + decode(came, scale, k)
        encode(whole[:rows, :], out, peaks)


def relay(came0, near0, came1, near1):
    rows, cols = max(near0.shape[0], near1.shape[0]), near0.shape[1]
    return pl.pallas_call(
        relay_body,
        out_shape=[jax.ShapeDtypeStruct(came.shape, jnp.int16) for came in (came0, came1)],
        scratch_shapes=[pltpu.VMEM((SROWS, cols), F32), pltpu.VMEM((rows, cols), F32)],
        compiler_params=pltpu.CompilerParams(vmem_limit_bytes=LIMIT),
        cost_estimate=pl.CostEstimate(flops=1, bytes_accessed=1, transcendentals=0),
        name="relay",
    )(came0, near0, came1, near1)


def fold_body(a, b, own, out, keep, peaks, other):
    rows = own.shape[0]
    sa, sb = scales(a, rows), scales(b, rows)
    for k in range(rows // BLK):
        span = slice(k * BLK, (k + 1) * BLK)
        total = own[span, :] + decode(a, sa, k) + decode(b, sb, k)
        keep[span, :] = total[:, : 2 * HW]
        other[span, :] = total[:, 2 * HW :]
    encode(other[...], out, peaks)


def fold(a, b, own):
    rows = own.shape[0]
    return pl.pallas_call(
        fold_body,
        out_shape=[
            jax.ShapeDtypeStruct((rows + SROWS, 2 * HW), jnp.int16),
            jax.ShapeDtypeStruct((rows, 2 * HW), F32),
        ],
        scratch_shapes=[pltpu.VMEM((SROWS, 2 * HW), F32), pltpu.VMEM((rows, 2 * HW), F32)],
        compiler_params=pltpu.CompilerParams(vmem_limit_bytes=LIMIT),
        cost_estimate=pl.CostEstimate(flops=1, bytes_accessed=1, transcendentals=0),
        name="fold",
    )(a, b, own)


def dispatch_body(parents, lengths, queries, table, send, turned, ropes, place, counts, spread):
    comps = queries.shape[0]
    group = queries.shape[1] // HW

    def look(c, carry):
        ropes[pl.ds(c, 1), :] = table[pl.ds(lengths[c] - 1, 1), :]
        return carry

    lax.fori_loop(0, comps, look, 0)
    for h in range(group):
        part = queries[:, h * HW : (h + 1) * HW].astype(F32)
        part = turn(part, ropes[:, :HW], ropes[:, HW:])
        turned[pl.ds(h, comps, stride=group), :] = part.astype(BF16).astype(F32)
    spread[...] = jnp.zeros(spread.shape, F32)

    def clear(i, carry):
        counts[i] = 0
        return carry

    lax.fori_loop(0, counts.shape[0], clear, 0)

    def put(c, carry):
        p = parents[c]
        s = counts[p]
        counts[p] = s + 1
        at = 2 * p + s
        place[c] = at
        to = pl.multiple_of(at * group, group)
        spread[pl.ds(to, group), :] = turned[pl.ds(pl.multiple_of(c * group, group), group), :]
        return carry

    lax.fori_loop(0, comps, put, 0)
    send[...] = spread[...].astype(BF16).reshape(send.shape)


def dispatch(parents, lengths, queries, table, prompts):
    comps = queries.shape[0]
    group = queries.shape[1] // HW
    vmem = pl.BlockSpec(memory_space=pltpu.VMEM)
    smem = pl.BlockSpec(memory_space=pltpu.SMEM)
    return pl.pallas_call(
        dispatch_body,
        in_specs=[smem, smem, vmem, vmem],
        out_specs=[vmem, vmem, vmem, smem],
        out_shape=[
            jax.ShapeDtypeStruct((prompts, 2 * group, HW), BF16),
            jax.ShapeDtypeStruct((comps * group, HW), F32),
            jax.ShapeDtypeStruct((comps, 2 * HW), F32),
            jax.ShapeDtypeStruct((comps,), jnp.int32),
        ],
        scratch_shapes=[pltpu.SMEM((prompts,), jnp.int32), pltpu.VMEM((prompts * 2 * group, HW), F32)],
        compiler_params=pltpu.CompilerParams(vmem_limit_bytes=LIMIT),
        cost_estimate=pl.CostEstimate(flops=1, bytes_accessed=1, transcendentals=0),
        name="dispatch",
    )(parents, lengths, queries, table)


def suffix_body(lengths, turned, cache, came, keep, bias, ropes, latest, out, stats, scores, weights, whole):
    comps = ropes.shape[0]
    first = keep.shape[0] - comps
    group = turned.shape[0] // comps
    scale = HW ** -0.5
    whole[...] = keep[first:, :] + bias[...] + decode(came, scales(came, keep.shape[0]), first // BLK)
    key = turn(whole[:, :HW], ropes[:, :HW], ropes[:, HW:]).astype(BF16)
    value = whole[:, HW:].astype(BF16)
    latest[:, :HW] = key
    latest[:, HW:] = value

    def wide(rows):
        return jnp.broadcast_to(rows[:, None, :], (comps, group, HW)).reshape(comps * group, HW)

    slot = lax.broadcasted_iota(jnp.int32, (group, HW), 1)
    for c in range(comps):
        span = slice(c * group, (c + 1) * group)
        score = nt(turned[span, :].astype(BF16), cache[c, :, :HW]) * scale
        scores[span, :] = jnp.where(slot < lengths[c], score, NEG)
    own_score = jnp.sum(turned[...] * wide(key.astype(F32)), axis=1, keepdims=True) * scale
    masked = scores[...]
    top = jnp.maximum(jnp.max(masked, axis=1, keepdims=True), own_score)
    weight = jnp.exp(masked - top)
    own_weight = jnp.exp(own_score - top)
    total = jnp.sum(weight, axis=1, keepdims=True) + own_weight
    weights[...] = weight
    for c in range(comps):
        span = slice(c * group, (c + 1) * group)
        out[span, :] = nn(weights[span, :].astype(BF16), cache[c, :, HW:])
    out[...] = out[...] + own_weight.astype(BF16).astype(F32) * wide(value.astype(F32))
    lane = lax.broadcasted_iota(jnp.int32, stats.shape, 1)
    stats[...] = jnp.where(lane < HW // 2, top, total)


def suffix(lengths, turned, cache, came, keep, bias, ropes):
    comps = ropes.shape[0]
    rows = turned.shape[0]
    vmem = pl.BlockSpec(memory_space=pltpu.VMEM)
    return pl.pallas_call(
        suffix_body,
        in_specs=[pl.BlockSpec(memory_space=pltpu.SMEM)] + [vmem] * 6,
        out_shape=[
            jax.ShapeDtypeStruct((comps, 2 * HW), BF16),
            jax.ShapeDtypeStruct((rows, HW), F32),
            jax.ShapeDtypeStruct((rows, HW), F32),
        ],
        scratch_shapes=[pltpu.VMEM((rows, HW), F32), pltpu.VMEM((rows, HW), F32), pltpu.VMEM((comps, 2 * HW), F32)],
        compiler_params=pltpu.CompilerParams(vmem_limit_bytes=LIMIT),
        cost_estimate=pl.CostEstimate(flops=10**7, bytes_accessed=10**7, transcendentals=0),
        name="suffix",
    )(lengths, turned, cache, came, keep, bias, ropes)


def prefix_body(queries, bias, turns, *refs):
    chunks = len(PARTS)
    came, keep = refs[:chunks], refs[chunks : 2 * chunks]
    kv, out = refs[2 * chunks :]
    blocks = kv.shape[0] // BLK
    cos_in, sin_in = turns[blocks:, :HW], turns[blocks:, HW:]
    for i, (first, rows) in enumerate(PARTS):
        scale = scales(came[i], keep[i].shape[0])
        for k in range(rows // BLK):
            span = slice(first + k * BLK, first + (k + 1) * BLK)
            total = keep[i][k * BLK : (k + 1) * BLK, :] + decode(came[i], scale, k) + bias[...]
            at = first // BLK + k
            cos_at, sin_at = turns[at : at + 1, :HW], turns[at : at + 1, HW:]
            cosine, sine = cos_at * cos_in - sin_at * sin_in, sin_at * cos_in + cos_at * sin_in
            kv[span, :HW] = turn(total[:, :HW], cosine, sine).astype(BF16)
            kv[span, HW:] = total[:, HW:].astype(BF16)
    prompts, per, _ = queries.shape
    step = 8
    for s in range(0, prompts, step):
        q = queries[s : s + step].reshape(step * per, HW)
        scores = nt(q, kv[:, :HW]) * (HW ** -0.5)
        top = jnp.max(scores, axis=1, keepdims=True)
        weight = jnp.exp(scores - top)
        total = jnp.sum(weight, axis=1, keepdims=True)
        part = nn(weight.astype(BF16), kv[:, HW:])
        peak = jnp.maximum(jnp.max(jnp.abs(part), axis=1, keepdims=True), 1e-30)
        level = jnp.ceil(jnp.log2(peak) * 256.0) + 1.0
        code = near_int(part * (jnp.exp2(level * (-1.0 / 256.0)) * QMAX))
        lane = lax.broadcasted_iota(jnp.int32, (step * per, HW), 1)
        row = lax.broadcasted_iota(jnp.int32, (step * per, HW), 0) % per
        stat = jnp.zeros((step * per, HW), F32)
        for i, piece in enumerate(pieces(top, TOP_STEPS) + pieces(total, TOTAL_STEPS) + [level]):
            stat = stat + jnp.where(lane == row + i * per, piece, 0.0)
        stat = jnp.sum(stat.reshape(step, per, HW), axis=1, keepdims=True)
        whole = jnp.concatenate([code.reshape(step, per, HW), jnp.broadcast_to(stat, (step, 8, HW))], axis=1)
        out[s : s + step] = whole.astype(jnp.int32).astype(jnp.int16)


def prefix(queries, bias, turns, came, keep, length):
    prompts, per, _ = queries.shape
    return pl.pallas_call(
        prefix_body,
        out_shape=[
            jax.ShapeDtypeStruct((length, 2 * HW), BF16),
            jax.ShapeDtypeStruct((prompts, per + 8, HW), jnp.int16),
        ],
        compiler_params=pltpu.CompilerParams(vmem_limit_bytes=LIMIT),
        cost_estimate=pl.CostEstimate(flops=2 * 10**8, bytes_accessed=10**7, transcendentals=10**6),
        name="prefix",
    )(queries, bias, turns, *came, *keep)


def merge_body(place, back, out, stats, attn, spread, side, joined):
    prompts, per, _ = back.shape
    per -= 8
    rows = out.shape[0]
    comps = attn.shape[0]
    group = rows // comps
    came = back[...].astype(jnp.int32).astype(F32)
    spread[...] = came
    for c in range(comps):
        at = place[c]
        span = slice(c * group, (c + 1) * group)
        slot = at % 2
        joined[span, :] = spread[at // 2, pl.ds(pl.multiple_of(slot * group, group), group), :]
        side[span, :] = jnp.where(
            lax.broadcasted_iota(jnp.int32, (group, HW), 1) % per
            == lax.broadcasted_iota(jnp.int32, (group, HW), 0) + slot * group,
            spread[at // 2, per:, :], 0.0)
    lane = lax.broadcasted_iota(jnp.int32, (rows, HW), 1)
    stat = []
    for i in range(len(TOP_STEPS) + len(TOTAL_STEPS) + 1):
        stat.append(jnp.sum(jnp.where(lane // per == i, side[...], 0.0), axis=1, keepdims=True))
    top_p = sum(piece * step for piece, step in zip(stat, TOP_STEPS))
    total_p = sum(piece * step for piece, step in zip(stat[len(TOP_STEPS) :], TOTAL_STEPS))
    out_p = joined[...] * (jnp.exp2(stat[-1] * (1.0 / 256.0)) * (1.0 / QMAX))
    top_s, total_s = stats[:, :1], stats[:, HW // 2 : HW // 2 + 1]
    top = jnp.maximum(top_p, top_s)
    alpha = jnp.exp(top_p - top)
    beta = jnp.exp(top_s - top)
    joined[...] = (alpha * out_p + beta * out[...]) / (alpha * total_p + beta * total_s)
    for h in range(group):
        attn[:, h * HW : (h + 1) * HW] = joined[pl.ds(h, comps, stride=group), :].astype(BF16)


def merge(place, back, out, stats, comps):
    rows = out.shape[0]
    vmem = pl.BlockSpec(memory_space=pltpu.VMEM)
    smem = pl.BlockSpec(memory_space=pltpu.SMEM)
    return pl.pallas_call(
        merge_body,
        in_specs=[smem, vmem, vmem, vmem],
        out_specs=vmem,
        out_shape=jax.ShapeDtypeStruct((comps, rows // comps * HW), BF16),
        scratch_shapes=[pltpu.VMEM(back.shape, F32), pltpu.VMEM((rows, HW), F32), pltpu.VMEM((rows, HW), F32)],
        compiler_params=pltpu.CompilerParams(vmem_limit_bytes=LIMIT),
        cost_estimate=pl.CostEstimate(flops=10**6, bytes_accessed=10**6, transcendentals=10**5),
        name="merge",
    )(place, back, out, stats)


def on_device(
    prefix_hidden_states, latest_hidden, queries, suffix_key_cache, key_value_weight, key_value_bias,
    adapter_down_weight, adapter_up_weight, parents, adapter_index, suffix_length_count,
):
    length = prefix_hidden_states.shape[1]
    comps = latest_hidden.shape[0]
    prompts = adapter_index.shape[0]
    along_y = lambda d: [(a * 2 + b, ((a + d) % 4) * 2 + b) for a in range(4) for b in range(2)]
    along_z = [(a * 2 + b, a * 2 + 1 - b) for a in range(4) for b in range(2)]

    hidden = prefix_hidden_states[0]
    y_step = lambda value, d: lax.ppermute(value, "tp", along_y(d))
    parent = parents[:, 0]
    in_hbm = lambda value: pltpu.with_memory_space_constraint(value, pltpu.HBM)
    hidden, key_value_weight, adapter_down_weight, adapter_up_weight, latest_hidden = map(
        in_hbm, (hidden, key_value_weight, adapter_down_weight, adapter_up_weight, latest_hidden))
    adapter_index, parent = in_hbm(adapter_index), in_hbm(parent)
    inputs = (adapter_index, parent, hidden, key_value_weight, adapter_down_weight, adapter_up_weight, latest_hidden)
    far0, far1, *known = project_far(FAR_LIMIT, *inputs)
    far0, far1 = y_step(far0, 1), y_step(far1, -1)
    direct0, direct1, near0, near1, own0, own1 = project_near(NEAR_LIMIT, *inputs, known)
    direct0, queries = lax.optimization_barrier((direct0, queries))

    cos_t, sin_t = rope_tables(length + 1, suffix_key_cache.shape[1])
    table = jnp.asarray(np.concatenate([cos_t, sin_t], 1))
    to_prompts, turned, ropes, place = dispatch(parent, suffix_length_count, queries, table, prompts)
    near0, near1, to_prompts = lax.optimization_barrier((near0, near1, to_prompts))
    joined0, joined1 = relay(far0, near0, far1, near1)
    joined0, joined1, to_prompts = lax.optimization_barrier((joined0, joined1, to_prompts))
    joined0, direct0 = y_step(joined0, 1), y_step(direct0, -1)
    joined1, direct1 = y_step(joined1, -1), y_step(direct1, 1)
    here = lax.all_to_all(to_prompts, "rep", 0, 0, tiled=True)
    joined0, direct0, here = lax.optimization_barrier((joined0, direct0, here))
    code0, keep0 = fold(joined0, direct0, own0)
    came0 = lax.ppermute(code0, "tp", along_z)
    code1, keep1 = fold(joined1, direct1, own1)
    came1 = lax.ppermute(code1, "tp", along_z)
    came, keep = (came0, came1), (keep0, keep1)

    bias = key_value_bias.astype(F32).reshape(1, 2 * HW)
    latest_key_value, out_s, stats = suffix(
        suffix_length_count, turned, in_hbm(suffix_key_cache), came[1], keep[1], bias, ropes)
    blocks, within = rope_tables(0, length, BLK), rope_tables(0, BLK)
    turns = jnp.asarray(np.concatenate([np.concatenate(blocks, 1), np.concatenate(within, 1)], 0))
    prefix_kv, part = prefix(here, bias, in_hbm(turns), came, keep, length)
    back = lax.all_to_all(part, "rep", 0, 0, tiled=True)
    attn_out = merge(place, back, out_s, stats, comps)
    return prefix_kv[None], latest_key_value, attn_out


def solution(mesh):
    in_specs = (
        P("rep", None, "tp"), P("rep", "tp"), P("rep", "tp"), P("rep", None, "tp"), P("tp", None), P("tp"),
        P("tp", None), P(), P("rep", None), P(), P("rep"),
    )
    out_specs = (P("rep", None, "tp"), P("rep", "tp"), P("rep", "tp"))
    return jax.shard_map(on_device, mesh=mesh, in_specs=in_specs, out_specs=out_specs, check_vma=False)
```

```python
import jax
import jax.numpy as jnp
import numpy as np
from jax import lax
from jax.experimental import pallas as pl
from jax.experimental.pallas import tpu as pltpu
from jax.sharding import PartitionSpec as P

HW = 128
RANK = 32
ROPE_BASE = 1000000.0
NEG = -1e30
PARTS = ((0, 416), (416, 352))
LIMIT = 16 * 2**20
FAR_LIMIT = 16 * 2**20
NEAR_LIMIT = 20 * 2**20
BLK = 32
SROWS = 16
QMAX = 32766.0
MAGIC = 12582912.0
TOP_STEPS = (2.0**12, 2.0**-3, 2.0**-18)
TOTAL_STEPS = (2.0**-5, 2.0**-20)
F32 = jnp.float32
BF16 = jnp.bfloat16


def rope_tables(first, count, step=1):
    half = HW // 2
    freq = (ROPE_BASE ** (-(np.arange(half, dtype=np.float64) * 2.0) / HW)).astype(np.float32)
    angle = np.arange(first, first + count, step, dtype=np.float32)[:, None] * freq[None, :]
    cosine = np.cos(angle.astype(np.float64)).astype(np.float32)
    sine = np.sin(angle.astype(np.float64)).astype(np.float32)
    return np.concatenate([cosine, cosine], 1), np.concatenate([-sine, sine], 1)


def turn(values, cosine, sine):
    return values * cosine + pltpu.roll(values, HW // 2, 1) * sine


def nn(a, b):
    return lax.dot_general(a, b, (((1,), (0,)), ((), ())), preferred_element_type=F32)


def nt(a, b):
    return lax.dot_general(a, b, (((1,), (1,)), ((), ())), preferred_element_type=F32)


def near_int(values):
    return (values + MAGIC) - MAGIC


def encode(values, out_ref, peak_ref):
    rows, cols = values.shape
    blocks = rows // BLK
    peak_ref[...] = jnp.full(peak_ref.shape, 1e-30, F32)
    for b in range(blocks):
        peak_ref[b : b + 1, :] = jnp.max(jnp.abs(values[b * BLK : (b + 1) * BLK]), axis=0, keepdims=True)
    level = jnp.ceil(jnp.log2(jnp.maximum(peak_ref[...], 1e-30)) * 256.0) + 1.0
    inverse = jnp.exp2(level * (-1.0 / 256.0)) * QMAX
    for b in range(blocks):
        scaled = values[b * BLK : (b + 1) * BLK] * inverse[b : b + 1, :]
        code = near_int(scaled)
        out_ref[b * BLK : (b + 1) * BLK, :] = code.astype(jnp.int32).astype(jnp.int16)
    out_ref[rows : rows + SROWS, :] = level.astype(jnp.int32).astype(jnp.int16)


def scales(ref, rows):
    level = ref[rows : rows + SROWS, :].astype(jnp.int32).astype(F32)
    return jnp.exp2(level * (1.0 / 256.0)) * (1.0 / QMAX)


def decode(ref, scale, b):
    return ref[b * BLK : (b + 1) * BLK, :].astype(jnp.int32).astype(F32) * scale[b : b + 1, :]


def pieces(value, steps):
    got = []
    for step in steps:
        whole = near_int(value * (1.0 / step))
        value = value - whole * step
        got.append(whole)
    return got


def spread_up(up, span, rows):
    key_row = (lax.broadcasted_iota(jnp.int32, (rows, HW), 0) % (2 * RANK)) < RANK
    zero = jnp.zeros((rows, HW), BF16)
    parts = []
    for other in range(2):
        part = up[span, other * HW : (other + 1) * HW]
        parts += [jnp.where(key_row, part, zero), jnp.where(key_row, zero, part)]
    return jnp.concatenate(parts, axis=1)


def two_parts(values):
    high = values.astype(BF16)
    return high, (values - high.astype(F32)).astype(BF16)


def project_body(offs, places, known, adapter_of, parents, hidden, weight, down, up, latest, *refs):
    if known:
        (xr_in, xl), refs = refs[:2], refs[2:]
        outs, (hx, wx, u, tile, peaks, sems) = refs[:-6], refs[-6:]
    else:
        outs, (xr_out, xl), (hx, wx, u, tile, peaks, dp, d, mine, sems) = refs[:-11], refs[-11:-9], refs[-9:]
    depth = hidden.shape[1]
    length, news = hidden.shape[0], latest.shape[0]
    (first0, rows0), (first1, rows1) = PARTS
    tp = lax.axis_index("tp")
    y, z = tp // 2, tp % 2
    adapter = adapter_of[lax.axis_index("rep")]
    pair = pl.ds(pl.multiple_of((adapter // 2) * (4 * RANK), 4 * RANK), 4 * RANK)

    def copy(src, dst, i):
        return pltpu.make_async_copy(src, dst, sems.at[i])

    blocks = []
    for k, off in enumerate(offs):
        made = []
        for other in range(2):
            head = ((y + off) % 4) * 2 + (1 - z if other else z)
            at = pl.ds(pl.multiple_of(head * (2 * HW), 2 * HW), 2 * HW)
            made.append(copy(weight.at[:, at], wx.at[k, pl.ds(0, depth), pl.ds(other * 2 * HW, 2 * HW)], 5 + 4 * k + other))
            at = pl.ds(pl.multiple_of(head * HW, HW), HW)
            made.append(copy(up.at[:, at], u.at[k, :, pl.ds(other * HW, HW)], 7 + 4 * k + other))
        blocks.append(made)
    early = [copy(hidden.at[pl.ds(first0, rows0), :], hx.at[pl.ds(first0, rows0), pl.ds(0, depth)], 1)]
    late = [
        copy(hidden.at[pl.ds(first1, rows1), :], hx.at[pl.ds(first1, rows1), pl.ds(0, depth)], 2),
        copy(latest, hx.at[pl.ds(length, news), pl.ds(0, depth)], 3),
    ]
    if known:
        hx[:, depth:] = xr_in[...]
    else:
        early.insert(0, copy(down.at[:, pair], dp, 0))
        late.append(copy(down, d, 4))
    for c in early + blocks[0] + late + [c for made in blocks[1:] for c in made]:
        c.start()

    if not known:
        def name(c, carry):
            mine[pl.ds(c, 1), :] = jnp.full((1, HW), adapter_of[parents[c]], jnp.int32)
            return carry

        lax.fori_loop(0, news, name, 0)
        hx[length:, depth:] = jnp.zeros((news, 8 * RANK), BF16)

    def ranks(first, rows):
        span = slice(first, first + rows)
        got = nn(hx[span, :depth], dp[...])
        lane = lax.broadcasted_iota(jnp.int32, got.shape, 1)
        high, low = two_parts(jnp.where((lane // (2 * RANK)) == adapter % 2, got, 0.0))
        hx[span, depth : depth + 4 * RANK] = high
        hx[span, depth + 4 * RANK :] = low

    def part0(k):
        for c in blocks[k]:
            c.wait()
        ups = spread_up(u.at[k], pair, 4 * RANK)
        wx[k, depth : depth + 4 * RANK, :] = ups
        wx[k, depth + 4 * RANK :, :] = ups
        emit(0, offs[k], nn(hx[:rows0, :], wx[k]))

    def emit(part, off, values):
        ref, coded = places(outs, part, off)
        if coded:
            tile[: values.shape[0], :] = values
            encode(tile[: values.shape[0], :], ref, peaks)
        else:
            ref[...] = values

    for c in early:
        c.wait()
    if not known:
        ranks(first0, rows0)
    part0(0)
    for c in late:
        c.wait()
    if not known:
        ranks(first1, rows1)
        got = nn(hx[length:, :depth], d[...])
        lane = lax.broadcasted_iota(jnp.int32, got.shape, 1)
        high, low = two_parts(jnp.where((lane // (2 * RANK)) == mine[:, :1], got, 0.0))
        xl[:news, :] = high
        xl[news:, :] = low
        xr_out[...] = hx[:, depth:]
    for k, off in enumerate(offs):
        if k:
            part0(k)
        added = nn(xl[...], spread_up(u.at[k], slice(None), up.shape[0]))
        ref, coded = places(outs, 1, off)
        to = tile if coded else ref
        to[: rows1 + news, :] = nn(hx[first1:, :], wx[k])
        to[rows1 : rows1 + news, :] = to[rows1 : rows1 + news, :] + (added[:news] + added[news:])
        if coded:
            encode(tile[: rows1 + news, :], ref, peaks)


def project_far(*args):
    return project((2,), lambda outs, part, off: (outs[part], True), 2, 0, *args, ())


def project_near(*args):
    table = {(0, 3): (0, True), (1, 1): (1, True), (0, 1): (2, False), (1, 3): (3, False), (0, 0): (4, False), (1, 0): (5, False)}

    def places(outs, part, off):
        at, coded = table[part, off]
        return outs[at], coded

    return project((3, 1, 0), places, 2, 4, *args)


def project(offs, places, codes, sums, limit, adapter_index, parents, hidden, weight, down, up, latest, known):
    depth = hidden.shape[1]
    length, news = hidden.shape[0], latest.shape[0]
    vmem = pl.BlockSpec(memory_space=pltpu.VMEM)
    hbm = pl.BlockSpec(memory_space=pltpu.HBM)
    smem = pl.BlockSpec(memory_space=pltpu.SMEM)
    rows = (PARTS[0][1], PARTS[1][1] + news)
    out_shape = [jax.ShapeDtypeStruct((rows[i % 2] + SROWS, 4 * HW), jnp.int16) for i in range(codes)]
    out_shape += [jax.ShapeDtypeStruct((rows[i % 2], 4 * HW), F32) for i in range(sums)]
    n = len(offs)
    ranks = [
        jax.ShapeDtypeStruct((length + news, 8 * RANK), BF16),
        jax.ShapeDtypeStruct((2 * news, up.shape[0]), BF16),
    ]
    if known:
        own = []
    else:
        out_shape += ranks
        own = [pltpu.VMEM((depth, 4 * RANK), BF16), pltpu.VMEM(down.shape, BF16), pltpu.VMEM((news, HW), jnp.int32)]
    return pl.pallas_call(
        lambda *refs: project_body(offs, places, bool(known), *refs),
        in_specs=[smem, smem] + [hbm] * 5 + [vmem] * len(known),
        out_specs=[vmem] * len(out_shape),
        out_shape=out_shape,
        scratch_shapes=[
            pltpu.VMEM((length + news, depth + 8 * RANK), BF16),
            pltpu.VMEM((n, depth + 8 * RANK, 4 * HW), BF16),
            pltpu.VMEM((n, up.shape[0], 2 * HW), BF16),
            pltpu.VMEM((max(rows), 4 * HW), F32),
            pltpu.VMEM((SROWS, 4 * HW), F32),
            *own,
            pltpu.SemaphoreType.DMA((5 + 4 * n,)),
        ],
        compiler_params=pltpu.CompilerParams(vmem_limit_bytes=limit),
        cost_estimate=pl.CostEstimate(
            flops=2 * length * depth * 4 * HW * n, bytes_accessed=2 * 10**6 * (n + 2), transcendentals=0),
        name="project%d" % n,
    )(adapter_index, parents, hidden, weight, down, up, latest, *known)


def relay_body(came0, near0, came1, near1, out0, out1, peaks, whole):
    for came, near, out in ((came0, near0, out0), (came1, near1, out1)):
        rows = near.shape[0]
        scale = scales(came, rows)
        for k in range(rows // BLK):
            span = slice(k * BLK, (k + 1) * BLK)
            whole[span, :] = near[span, :] + decode(came, scale, k)
        encode(whole[:rows, :], out, peaks)


def relay(came0, near0, came1, near1):
    rows, cols = max(near0.shape[0], near1.shape[0]), near0.shape[1]
    return pl.pallas_call(
        relay_body,
        out_shape=[jax.ShapeDtypeStruct(came.shape, jnp.int16) for came in (came0, came1)],
        input_output_aliases={0: 0, 2: 1},
        scratch_shapes=[pltpu.VMEM((SROWS, cols), F32), pltpu.VMEM((rows, cols), F32)],
        compiler_params=pltpu.CompilerParams(vmem_limit_bytes=LIMIT),
        cost_estimate=pl.CostEstimate(flops=1, bytes_accessed=1, transcendentals=0),
        name="relay",
    )(came0, near0, came1, near1)


def fold_body(a, b, own, out, keep, peaks, other):
    rows = own.shape[0]
    sa, sb = scales(a, rows), scales(b, rows)
    for k in range(rows // BLK):
        span = slice(k * BLK, (k + 1) * BLK)
        total = own[span, :] + decode(a, sa, k) + decode(b, sb, k)
        keep[span, :] = total[:, : 2 * HW]
        other[span, :] = total[:, 2 * HW :]
    encode(other[...], out, peaks)


def fold(a, b, own):
    rows = own.shape[0]
    return pl.pallas_call(
        fold_body,
        out_shape=[
            jax.ShapeDtypeStruct((rows + SROWS, 2 * HW), jnp.int16),
            jax.ShapeDtypeStruct((rows, 2 * HW), F32),
        ],
        scratch_shapes=[pltpu.VMEM((SROWS, 2 * HW), F32), pltpu.VMEM((rows, 2 * HW), F32)],
        compiler_params=pltpu.CompilerParams(vmem_limit_bytes=LIMIT),
        cost_estimate=pl.CostEstimate(flops=1, bytes_accessed=1, transcendentals=0),
        name="fold",
    )(a, b, own)


def dispatch_body(parents, lengths, queries, table, send, turned, ropes, place, counts, spread):
    comps = queries.shape[0]
    group = queries.shape[1] // HW

    def look(c, carry):
        ropes[pl.ds(c, 1), :] = table[pl.ds(lengths[c] - 1, 1), :]
        return carry

    lax.fori_loop(0, comps, look, 0)
    for h in range(group):
        part = queries[:, h * HW : (h + 1) * HW].astype(F32)
        part = turn(part, ropes[:, :HW], ropes[:, HW:])
        turned[pl.ds(h, comps, stride=group), :] = part.astype(BF16).astype(F32)
    spread[...] = jnp.zeros(spread.shape, F32)

    def clear(i, carry):
        counts[i] = 0
        return carry

    lax.fori_loop(0, counts.shape[0], clear, 0)

    def put(c, carry):
        p = parents[c]
        s = counts[p]
        counts[p] = s + 1
        at = 2 * p + s
        place[c] = at
        to = pl.multiple_of(at * group, group)
        spread[pl.ds(to, group), :] = turned[pl.ds(pl.multiple_of(c * group, group), group), :]
        return carry

    lax.fori_loop(0, comps, put, 0)
    send[...] = spread[...].astype(BF16).reshape(send.shape)


def dispatch(parents, lengths, queries, table, prompts):
    comps = queries.shape[0]
    group = queries.shape[1] // HW
    vmem = pl.BlockSpec(memory_space=pltpu.VMEM)
    smem = pl.BlockSpec(memory_space=pltpu.SMEM)
    return pl.pallas_call(
        dispatch_body,
        in_specs=[smem, smem, vmem, vmem],
        out_specs=[vmem, vmem, vmem, smem],
        out_shape=[
            jax.ShapeDtypeStruct((prompts, 2 * group, HW), BF16),
            jax.ShapeDtypeStruct((comps * group, HW), F32),
            jax.ShapeDtypeStruct((comps, 2 * HW), F32),
            jax.ShapeDtypeStruct((comps,), jnp.int32),
        ],
        scratch_shapes=[pltpu.SMEM((prompts,), jnp.int32), pltpu.VMEM((prompts * 2 * group, HW), F32)],
        compiler_params=pltpu.CompilerParams(vmem_limit_bytes=LIMIT),
        cost_estimate=pl.CostEstimate(flops=1, bytes_accessed=1, transcendentals=0),
        name="dispatch",
    )(parents, lengths, queries, table)


def suffix_body(lengths, turned, cache, came, keep, bias, ropes, latest, out, stats, scores, weights, whole):
    comps = ropes.shape[0]
    first = keep.shape[0] - comps
    group = turned.shape[0] // comps
    scale = HW ** -0.5
    whole[...] = keep[first:, :] + bias[...] + decode(came, scales(came, keep.shape[0]), first // BLK)
    key = turn(whole[:, :HW], ropes[:, :HW], ropes[:, HW:]).astype(BF16)
    value = whole[:, HW:].astype(BF16)
    latest[:, :HW] = key
    latest[:, HW:] = value

    def wide(rows):
        return jnp.broadcast_to(rows[:, None, :], (comps, group, HW)).reshape(comps * group, HW)

    slot = lax.broadcasted_iota(jnp.int32, (group, HW), 1)
    for c in range(comps):
        span = slice(c * group, (c + 1) * group)
        score = nt(turned[span, :].astype(BF16), cache[c, :, :HW]) * scale
        scores[span, :] = jnp.where(slot < lengths[c], score, NEG)
    own_score = jnp.sum(turned[...] * wide(key.astype(F32)), axis=1, keepdims=True) * scale
    masked = scores[...]
    top = jnp.maximum(jnp.max(masked, axis=1, keepdims=True), own_score)
    weight = jnp.exp(masked - top)
    own_weight = jnp.exp(own_score - top)
    total = jnp.sum(weight, axis=1, keepdims=True) + own_weight
    weights[...] = weight
    for c in range(comps):
        span = slice(c * group, (c + 1) * group)
        out[span, :] = nn(weights[span, :].astype(BF16), cache[c, :, HW:])
    out[...] = out[...] + own_weight.astype(BF16).astype(F32) * wide(value.astype(F32))
    lane = lax.broadcasted_iota(jnp.int32, stats.shape, 1)
    stats[...] = jnp.where(lane < HW // 2, top, total)


def suffix(lengths, turned, cache, came, keep, bias, ropes):
    comps = ropes.shape[0]
    rows = turned.shape[0]
    vmem = pl.BlockSpec(memory_space=pltpu.VMEM)
    return pl.pallas_call(
        suffix_body,
        in_specs=[pl.BlockSpec(memory_space=pltpu.SMEM)] + [vmem] * 6,
        out_shape=[
            jax.ShapeDtypeStruct((comps, 2 * HW), BF16),
            jax.ShapeDtypeStruct((rows, HW), F32),
            jax.ShapeDtypeStruct((rows, HW), F32),
        ],
        scratch_shapes=[pltpu.VMEM((rows, HW), F32), pltpu.VMEM((rows, HW), F32), pltpu.VMEM((comps, 2 * HW), F32)],
        compiler_params=pltpu.CompilerParams(vmem_limit_bytes=LIMIT),
        cost_estimate=pl.CostEstimate(flops=10**7, bytes_accessed=10**7, transcendentals=0),
        name="suffix",
    )(lengths, turned, cache, came, keep, bias, ropes)


def prefix_body(queries, bias, turns, *refs):
    chunks = len(PARTS)
    came, keep = refs[:chunks], refs[chunks : 2 * chunks]
    kv, out = refs[2 * chunks :]
    blocks = kv.shape[0] // BLK
    cos_in, sin_in = turns[blocks:, :HW], turns[blocks:, HW:]
    for i, (first, rows) in enumerate(PARTS):
        scale = scales(came[i], keep[i].shape[0])
        for k in range(rows // BLK):
            span = slice(first + k * BLK, first + (k + 1) * BLK)
            total = keep[i][k * BLK : (k + 1) * BLK, :] + decode(came[i], scale, k) + bias[...]
            at = first // BLK + k
            cos_at, sin_at = turns[at : at + 1, :HW], turns[at : at + 1, HW:]
            cosine, sine = cos_at * cos_in - sin_at * sin_in, sin_at * cos_in + cos_at * sin_in
            kv[span, :HW] = turn(total[:, :HW], cosine, sine).astype(BF16)
            kv[span, HW:] = total[:, HW:].astype(BF16)
    prompts, per, _ = queries.shape
    step = 16
    for s in range(0, prompts, step):
        q = queries[s : s + step].reshape(step * per, HW)
        scores = nt(q, kv[:, :HW]) * (HW ** -0.5)
        top = jnp.max(scores, axis=1, keepdims=True)
        weight = jnp.exp(scores - top)
        total = jnp.sum(weight, axis=1, keepdims=True)
        part = nn(weight.astype(BF16), kv[:, HW:])
        peak = jnp.maximum(jnp.max(jnp.abs(part), axis=1, keepdims=True), 1e-30)
        level = jnp.ceil(jnp.log2(peak) * 256.0) + 1.0
        code = near_int(part * (jnp.exp2(level * (-1.0 / 256.0)) * QMAX))
        lane = lax.broadcasted_iota(jnp.int32, (step * per, HW), 1)
        row = lax.broadcasted_iota(jnp.int32, (step * per, HW), 0) % per
        stat = jnp.zeros((step * per, HW), F32)
        for i, piece in enumerate(pieces(top, TOP_STEPS) + pieces(total, TOTAL_STEPS) + [level]):
            stat = stat + jnp.where(lane == row + i * per, piece, 0.0)
        stat = jnp.sum(stat.reshape(step, per, HW), axis=1, keepdims=True)
        whole = jnp.concatenate([code.reshape(step, per, HW), jnp.broadcast_to(stat, (step, 8, HW))], axis=1)
        out[s : s + step] = whole.astype(jnp.int32).astype(jnp.int16)


def prefix(queries, bias, turns, came, keep, length):
    prompts, per, _ = queries.shape
    return pl.pallas_call(
        prefix_body,
        out_shape=[
            jax.ShapeDtypeStruct((length, 2 * HW), BF16),
            jax.ShapeDtypeStruct((prompts, per + 8, HW), jnp.int16),
        ],
        compiler_params=pltpu.CompilerParams(vmem_limit_bytes=LIMIT),
        cost_estimate=pl.CostEstimate(flops=2 * 10**8, bytes_accessed=10**7, transcendentals=10**6),
        name="prefix",
    )(queries, bias, turns, *came, *keep)


def merge_body(place, back, out, stats, attn, spread, side, joined):
    prompts, per, _ = back.shape
    per -= 8
    rows = out.shape[0]
    comps = attn.shape[0]
    group = rows // comps
    came = back[...].astype(jnp.int32).astype(F32)
    spread[...] = came
    for c in range(comps):
        at = place[c]
        span = slice(c * group, (c + 1) * group)
        slot = at % 2
        joined[span, :] = spread[at // 2, pl.ds(pl.multiple_of(slot * group, group), group), :]
        side[span, :] = jnp.where(
            lax.broadcasted_iota(jnp.int32, (group, HW), 1) % per
            == lax.broadcasted_iota(jnp.int32, (group, HW), 0) + slot * group,
            spread[at // 2, per:, :], 0.0)
    lane = lax.broadcasted_iota(jnp.int32, (rows, HW), 1)
    stat = []
    for i in range(len(TOP_STEPS) + len(TOTAL_STEPS) + 1):
        stat.append(jnp.sum(jnp.where(lane // per == i, side[...], 0.0), axis=1, keepdims=True))
    top_p = sum(piece * step for piece, step in zip(stat, TOP_STEPS))
    total_p = sum(piece * step for piece, step in zip(stat[len(TOP_STEPS) :], TOTAL_STEPS))
    out_p = joined[...] * (jnp.exp2(stat[-1] * (1.0 / 256.0)) * (1.0 / QMAX))
    top_s, total_s = stats[:, :1], stats[:, HW // 2 : HW // 2 + 1]
    top = jnp.maximum(top_p, top_s)
    alpha = jnp.exp(top_p - top)
    beta = jnp.exp(top_s - top)
    joined[...] = (alpha * out_p + beta * out[...]) / (alpha * total_p + beta * total_s)
    for h in range(group):
        attn[:, h * HW : (h + 1) * HW] = joined[pl.ds(h, comps, stride=group), :].astype(BF16)


def merge(place, back, out, stats, comps):
    rows = out.shape[0]
    vmem = pl.BlockSpec(memory_space=pltpu.VMEM)
    smem = pl.BlockSpec(memory_space=pltpu.SMEM)
    return pl.pallas_call(
        merge_body,
        in_specs=[smem, vmem, vmem, vmem],
        out_specs=vmem,
        out_shape=jax.ShapeDtypeStruct((comps, rows // comps * HW), BF16),
        scratch_shapes=[pltpu.VMEM(back.shape, F32), pltpu.VMEM((rows, HW), F32), pltpu.VMEM((rows, HW), F32)],
        compiler_params=pltpu.CompilerParams(vmem_limit_bytes=LIMIT),
        cost_estimate=pl.CostEstimate(flops=10**6, bytes_accessed=10**6, transcendentals=10**5),
        name="merge",
    )(place, back, out, stats)


def on_device(
    prefix_hidden_states, latest_hidden, queries, suffix_key_cache, key_value_weight, key_value_bias,
    adapter_down_weight, adapter_up_weight, parents, adapter_index, suffix_length_count,
):
    length = prefix_hidden_states.shape[1]
    comps = latest_hidden.shape[0]
    prompts = adapter_index.shape[0]
    along_y = lambda d: [(a * 2 + b, ((a + d) % 4) * 2 + b) for a in range(4) for b in range(2)]
    along_z = [(a * 2 + b, a * 2 + 1 - b) for a in range(4) for b in range(2)]

    hidden = prefix_hidden_states[0]
    y_step = lambda value, d: lax.ppermute(value, "tp", along_y(d))
    parent = parents[:, 0]
    in_hbm = lambda value: pltpu.with_memory_space_constraint(value, pltpu.HBM)
    hidden, key_value_weight, adapter_down_weight, adapter_up_weight, latest_hidden = map(
        in_hbm, (hidden, key_value_weight, adapter_down_weight, adapter_up_weight, latest_hidden))
    adapter_index, parent = in_hbm(adapter_index), in_hbm(parent)
    inputs = (adapter_index, parent, hidden, key_value_weight, adapter_down_weight, adapter_up_weight, latest_hidden)
    far0, far1, *known = project_far(FAR_LIMIT, *inputs)
    far0, far1 = y_step(far0, 1), y_step(far1, -1)
    direct0, direct1, near0, near1, own0, own1 = project_near(NEAR_LIMIT, *inputs, known)
    direct0, queries = lax.optimization_barrier((direct0, queries))

    cos_t, sin_t = rope_tables(length + 1, suffix_key_cache.shape[1])
    table = jnp.asarray(np.concatenate([cos_t, sin_t], 1))
    to_prompts, turned, ropes, place = dispatch(parent, suffix_length_count, queries, table, prompts)
    near0, near1, to_prompts = lax.optimization_barrier((near0, near1, to_prompts))
    joined0, joined1 = relay(far0, near0, far1, near1)
    joined0, joined1, to_prompts = lax.optimization_barrier((joined0, joined1, to_prompts))
    joined0, direct0 = y_step(joined0, 1), y_step(direct0, -1)
    joined1, direct1 = y_step(joined1, -1), y_step(direct1, 1)
    here = lax.all_to_all(to_prompts, "rep", 0, 0, tiled=True)
    code0, keep0 = fold(joined0, direct0, own0)
    came0 = lax.ppermute(code0, "tp", along_z)
    code1, keep1 = fold(joined1, direct1, own1)
    came1 = lax.ppermute(code1, "tp", along_z)
    came, keep = (came0, came1), (keep0, keep1)

    bias = key_value_bias.astype(F32).reshape(1, 2 * HW)
    latest_key_value, out_s, stats = suffix(
        suffix_length_count, turned, in_hbm(suffix_key_cache), came[1], keep[1], bias, ropes)
    blocks, within = rope_tables(0, length, BLK), rope_tables(0, BLK)
    turns = jnp.asarray(np.concatenate([np.concatenate(blocks, 1), np.concatenate(within, 1)], 0))
    prefix_kv, part = prefix(here, bias, in_hbm(turns), came, keep, length)
    back = lax.all_to_all(part, "rep", 0, 0, tiled=True)
    attn_out = merge(place, back, out_s, stats, comps)
    return prefix_kv[None], latest_key_value, attn_out


def solution(mesh):
    in_specs = (
        P("rep", None, "tp"), P("rep", "tp"), P("rep", "tp"), P("rep", None, "tp"), P("tp", None), P("tp"),
        P("tp", None), P(), P("rep", None), P(), P("rep"),
    )
    out_specs = (P("rep", None, "tp"), P("rep", "tp"), P("rep", "tp"))
    return jax.shard_map(on_device, mesh=mesh, in_specs=in_specs, out_specs=out_specs, check_vma=False)
```

```python
import jax
import jax.numpy as jnp
import numpy as np
from jax import lax
from jax.experimental import pallas as pl
from jax.experimental.pallas import tpu as pltpu
from jax.sharding import PartitionSpec as P

HW = 128
RANK = 32
ROPE_BASE = 1000000.0
NEG = -1e30
PARTS = ((0, 416), (416, 352))
LIMIT = 16 * 2**20
FAR_LIMIT = 16 * 2**20
NEAR_LIMIT = 20 * 2**20
BLK = 32
SROWS = 16
QMAX = 32766.0
MAGIC = 12582912.0
TOP_STEPS = (2.0**12, 2.0**-3, 2.0**-18)
TOTAL_STEPS = (2.0**-5, 2.0**-20)
F32 = jnp.float32
BF16 = jnp.bfloat16


def rope_tables(first, count, step=1):
    half = HW // 2
    freq = (ROPE_BASE ** (-(np.arange(half, dtype=np.float64) * 2.0) / HW)).astype(np.float32)
    angle = np.arange(first, first + count, step, dtype=np.float32)[:, None] * freq[None, :]
    cosine = np.cos(angle.astype(np.float64)).astype(np.float32)
    sine = np.sin(angle.astype(np.float64)).astype(np.float32)
    return np.concatenate([cosine, cosine], 1), np.concatenate([-sine, sine], 1)


def turn(values, cosine, sine):
    return values * cosine + pltpu.roll(values, HW // 2, 1) * sine


def nn(a, b):
    return lax.dot_general(a, b, (((1,), (0,)), ((), ())), preferred_element_type=F32)


def nt(a, b):
    return lax.dot_general(a, b, (((1,), (1,)), ((), ())), preferred_element_type=F32)


def near_int(values):
    return (values + MAGIC) - MAGIC


def encode(values, out_ref, peak_ref):
    rows, cols = values.shape
    blocks = rows // BLK
    peak_ref[...] = jnp.full(peak_ref.shape, 1e-30, F32)
    for b in range(blocks):
        peak_ref[b : b + 1, :] = jnp.max(jnp.abs(values[b * BLK : (b + 1) * BLK]), axis=0, keepdims=True)
    level = jnp.ceil(jnp.log2(jnp.maximum(peak_ref[...], 1e-30)) * 256.0) + 1.0
    inverse = jnp.exp2(level * (-1.0 / 256.0)) * QMAX
    for b in range(blocks):
        scaled = values[b * BLK : (b + 1) * BLK] * inverse[b : b + 1, :]
        code = near_int(scaled)
        out_ref[b * BLK : (b + 1) * BLK, :] = code.astype(jnp.int32).astype(jnp.int16)
    out_ref[rows : rows + SROWS, :] = level.astype(jnp.int32).astype(jnp.int16)


def scales(ref, rows):
    level = ref[rows : rows + SROWS, :].astype(jnp.int32).astype(F32)
    return jnp.exp2(level * (1.0 / 256.0)) * (1.0 / QMAX)


def decode(ref, scale, b):
    return ref[b * BLK : (b + 1) * BLK, :].astype(jnp.int32).astype(F32) * scale[b : b + 1, :]


def pieces(value, steps):
    got = []
    for step in steps:
        whole = near_int(value * (1.0 / step))
        value = value - whole * step
        got.append(whole)
    return got


def spread_up(up, span, rows):
    key_row = (lax.broadcasted_iota(jnp.int32, (rows, HW), 0) % (2 * RANK)) < RANK
    zero = jnp.zeros((rows, HW), BF16)
    parts = []
    for other in range(2):
        part = up[span, other * HW : (other + 1) * HW]
        parts += [jnp.where(key_row, part, zero), jnp.where(key_row, zero, part)]
    return jnp.concatenate(parts, axis=1)


def two_parts(values):
    high = values.astype(BF16)
    return high, (values - high.astype(F32)).astype(BF16)


def project_body(offs, places, known, adapter_of, parents, hidden, weight, down, up, latest, *refs):
    if known:
        (xr_in, xl), refs = refs[:2], refs[2:]
        outs, (hx, wx, u, tile, peaks, sems) = refs[:-6], refs[-6:]
    else:
        outs, (xr_out, xl), (hx, wx, u, tile, peaks, dp, d, mine, sems) = refs[:-11], refs[-11:-9], refs[-9:]
    depth = hidden.shape[1]
    length, news = hidden.shape[0], latest.shape[0]
    (first0, rows0), (first1, rows1) = PARTS
    tp = lax.axis_index("tp")
    y, z = tp // 2, tp % 2
    adapter = adapter_of[lax.axis_index("rep")]
    pair = pl.ds(pl.multiple_of((adapter // 2) * (4 * RANK), 4 * RANK), 4 * RANK)

    def copy(src, dst, i):
        return pltpu.make_async_copy(src, dst, sems.at[i])

    blocks = []
    for k, off in enumerate(offs):
        made = []
        for other in range(2):
            head = ((y + off) % 4) * 2 + (1 - z if other else z)
            at = pl.ds(pl.multiple_of(head * (2 * HW), 2 * HW), 2 * HW)
            made.append(copy(weight.at[:, at], wx.at[k, pl.ds(0, depth), pl.ds(other * 2 * HW, 2 * HW)], 5 + 4 * k + other))
            at = pl.ds(pl.multiple_of(head * HW, HW), HW)
            made.append(copy(up.at[:, at], u.at[k, :, pl.ds(other * HW, HW)], 7 + 4 * k + other))
        blocks.append(made)
    early = [copy(hidden.at[pl.ds(first0, rows0), :], hx.at[pl.ds(first0, rows0), pl.ds(0, depth)], 1)]
    late = [
        copy(hidden.at[pl.ds(first1, rows1), :], hx.at[pl.ds(first1, rows1), pl.ds(0, depth)], 2),
        copy(latest, hx.at[pl.ds(length, news), pl.ds(0, depth)], 3),
    ]
    if known:
        hx[:, depth:] = xr_in[...]
    else:
        early.insert(0, copy(down.at[:, pair], dp, 0))
        late.append(copy(down, d, 4))
    for c in early + blocks[0] + late + [c for made in blocks[1:] for c in made]:
        c.start()

    if not known:
        def name(c, carry):
            mine[pl.ds(c, 1), :] = jnp.full((1, HW), adapter_of[parents[c]], jnp.int32)
            return carry

        lax.fori_loop(0, news, name, 0)
        hx[length:, depth:] = jnp.zeros((news, 8 * RANK), BF16)

    def ranks(first, rows):
        span = slice(first, first + rows)
        got = nn(hx[span, :depth], dp[...])
        lane = lax.broadcasted_iota(jnp.int32, got.shape, 1)
        high, low = two_parts(jnp.where((lane // (2 * RANK)) == adapter % 2, got, 0.0))
        hx[span, depth : depth + 4 * RANK] = high
        hx[span, depth + 4 * RANK :] = low

    def part0(k):
        for c in blocks[k]:
            c.wait()
        ups = spread_up(u.at[k], pair, 4 * RANK)
        wx[k, depth : depth + 4 * RANK, :] = ups
        wx[k, depth + 4 * RANK :, :] = ups
        emit(0, offs[k], nn(hx[:rows0, :], wx[k]))

    def emit(part, off, values):
        ref, coded = places(outs, part, off)
        if coded:
            tile[: values.shape[0], :] = values
            encode(tile[: values.shape[0], :], ref, peaks)
        else:
            ref[...] = values

    for c in early:
        c.wait()
    if not known:
        ranks(first0, rows0)
    part0(0)
    for c in late:
        c.wait()
    if not known:
        ranks(first1, rows1)
        got = nn(hx[length:, :depth], d[...])
        lane = lax.broadcasted_iota(jnp.int32, got.shape, 1)
        high, low = two_parts(jnp.where((lane // (2 * RANK)) == mine[:, :1], got, 0.0))
        xl[:news, :] = high
        xl[news:, :] = low
        xr_out[...] = hx[:, depth:]
    for k, off in enumerate(offs):
        if k:
            part0(k)
        added = nn(xl[...], spread_up(u.at[k], slice(None), up.shape[0]))
        ref, coded = places(outs, 1, off)
        to = tile if coded else ref
        to[: rows1 + news, :] = nn(hx[first1:, :], wx[k])
        to[rows1 : rows1 + news, :] = to[rows1 : rows1 + news, :] + (added[:news] + added[news:])
        if coded:
            encode(tile[: rows1 + news, :], ref, peaks)


def project_far(*args):
    return project((2,), lambda outs, part, off: (outs[part], True), 2, 0, *args, ())


def project_near(*args):
    table = {(0, 3): (0, True), (1, 1): (1, True), (0, 1): (2, False), (1, 3): (3, False), (0, 0): (4, False), (1, 0): (5, False)}

    def places(outs, part, off):
        at, coded = table[part, off]
        return outs[at], coded

    return project((3, 1, 0), places, 2, 4, *args)


def project(offs, places, codes, sums, limit, adapter_index, parents, hidden, weight, down, up, latest, known):
    depth = hidden.shape[1]
    length, news = hidden.shape[0], latest.shape[0]
    vmem = pl.BlockSpec(memory_space=pltpu.VMEM)
    hbm = pl.BlockSpec(memory_space=pltpu.HBM)
    smem = pl.BlockSpec(memory_space=pltpu.SMEM)
    rows = (PARTS[0][1], PARTS[1][1] + news)
    out_shape = [jax.ShapeDtypeStruct((rows[i % 2] + SROWS, 4 * HW), jnp.int16) for i in range(codes)]
    out_shape += [jax.ShapeDtypeStruct((rows[i % 2], 4 * HW), F32) for i in range(sums)]
    n = len(offs)
    ranks = [
        jax.ShapeDtypeStruct((length + news, 8 * RANK), BF16),
        jax.ShapeDtypeStruct((2 * news, up.shape[0]), BF16),
    ]
    if known:
        own = []
    else:
        out_shape += ranks
        own = [pltpu.VMEM((depth, 4 * RANK), BF16), pltpu.VMEM(down.shape, BF16), pltpu.VMEM((news, HW), jnp.int32)]
    return pl.pallas_call(
        lambda *refs: project_body(offs, places, bool(known), *refs),
        in_specs=[smem, smem] + [hbm] * 5 + [vmem] * len(known),
        out_specs=[vmem] * len(out_shape),
        out_shape=out_shape,
        scratch_shapes=[
            pltpu.VMEM((length + news, depth + 8 * RANK), BF16),
            pltpu.VMEM((n, depth + 8 * RANK, 4 * HW), BF16),
            pltpu.VMEM((n, up.shape[0], 2 * HW), BF16),
            pltpu.VMEM((max(rows), 4 * HW), F32),
            pltpu.VMEM((SROWS, 4 * HW), F32),
            *own,
            pltpu.SemaphoreType.DMA((5 + 4 * n,)),
        ],
        compiler_params=pltpu.CompilerParams(vmem_limit_bytes=limit),
        cost_estimate=pl.CostEstimate(
            flops=2 * length * depth * 4 * HW * n, bytes_accessed=2 * 10**6 * (n + 2), transcendentals=0),
        name="project%d" % n,
    )(adapter_index, parents, hidden, weight, down, up, latest, *known)


def relay_body(came, near, out, peaks, whole):
    rows = near.shape[0]
    scale = scales(came, rows)
    for k in range(rows // BLK):
        span = slice(k * BLK, (k + 1) * BLK)
        whole[span, :] = near[span, :] + decode(came, scale, k)
    encode(whole[...], out, peaks)


def relay(came, near):
    rows, cols = near.shape
    return pl.pallas_call(
        relay_body,
        out_shape=jax.ShapeDtypeStruct(came.shape, jnp.int16),
        input_output_aliases={0: 0},
        scratch_shapes=[pltpu.VMEM((SROWS, cols), F32), pltpu.VMEM((rows, cols), F32)],
        compiler_params=pltpu.CompilerParams(vmem_limit_bytes=LIMIT),
        cost_estimate=pl.CostEstimate(flops=1, bytes_accessed=1, transcendentals=0),
        name="relay",
    )(came, near)


def fold_body(a, b, own, out, keep, peaks, other):
    rows = own.shape[0]
    sa, sb = scales(a, rows), scales(b, rows)
    for k in range(rows // BLK):
        span = slice(k * BLK, (k + 1) * BLK)
        total = own[span, :] + decode(a, sa, k) + decode(b, sb, k)
        keep[span, :] = total[:, : 2 * HW]
        other[span, :] = total[:, 2 * HW :]
    encode(other[...], out, peaks)


def fold(a, b, own):
    rows = own.shape[0]
    return pl.pallas_call(
        fold_body,
        out_shape=[
            jax.ShapeDtypeStruct((rows + SROWS, 2 * HW), jnp.int16),
            jax.ShapeDtypeStruct((rows, 2 * HW), F32),
        ],
        scratch_shapes=[pltpu.VMEM((SROWS, 2 * HW), F32), pltpu.VMEM((rows, 2 * HW), F32)],
        compiler_params=pltpu.CompilerParams(vmem_limit_bytes=LIMIT),
        cost_estimate=pl.CostEstimate(flops=1, bytes_accessed=1, transcendentals=0),
        name="fold",
    )(a, b, own)


def dispatch_body(parents, lengths, queries, table, send, turned, ropes, place, counts, spread):
    comps = queries.shape[0]
    group = queries.shape[1] // HW

    def look(c, carry):
        ropes[pl.ds(c, 1), :] = table[pl.ds(lengths[c] - 1, 1), :]
        return carry

    lax.fori_loop(0, comps, look, 0)
    for h in range(group):
        part = queries[:, h * HW : (h + 1) * HW].astype(F32)
        part = turn(part, ropes[:, :HW], ropes[:, HW:])
        turned[pl.ds(h, comps, stride=group), :] = part.astype(BF16).astype(F32)
    spread[...] = jnp.zeros(spread.shape, F32)

    def clear(i, carry):
        counts[i] = 0
        return carry

    lax.fori_loop(0, counts.shape[0], clear, 0)

    def put(c, carry):
        p = parents[c]
        s = counts[p]
        counts[p] = s + 1
        at = 2 * p + s
        place[c] = at
        to = pl.multiple_of(at * group, group)
        spread[pl.ds(to, group), :] = turned[pl.ds(pl.multiple_of(c * group, group), group), :]
        return carry

    lax.fori_loop(0, comps, put, 0)
    send[...] = spread[...].astype(BF16).reshape(send.shape)


def dispatch(parents, lengths, queries, table, prompts):
    comps = queries.shape[0]
    group = queries.shape[1] // HW
    vmem = pl.BlockSpec(memory_space=pltpu.VMEM)
    smem = pl.BlockSpec(memory_space=pltpu.SMEM)
    return pl.pallas_call(
        dispatch_body,
        in_specs=[smem, smem, vmem, vmem],
        out_specs=[vmem, vmem, vmem, smem],
        out_shape=[
            jax.ShapeDtypeStruct((prompts, 2 * group, HW), BF16),
            jax.ShapeDtypeStruct((comps * group, HW), F32),
            jax.ShapeDtypeStruct((comps, 2 * HW), F32),
            jax.ShapeDtypeStruct((comps,), jnp.int32),
        ],
        scratch_shapes=[pltpu.SMEM((prompts,), jnp.int32), pltpu.VMEM((prompts * 2 * group, HW), F32)],
        compiler_params=pltpu.CompilerParams(vmem_limit_bytes=LIMIT),
        cost_estimate=pl.CostEstimate(flops=1, bytes_accessed=1, transcendentals=0),
        name="dispatch",
    )(parents, lengths, queries, table)


def suffix_body(lengths, turned, cache, came, keep, bias, ropes, latest, out, stats, scores, weights, whole):
    comps = ropes.shape[0]
    first = keep.shape[0] - comps
    group = turned.shape[0] // comps
    scale = HW ** -0.5
    whole[...] = keep[first:, :] + bias[...] + decode(came, scales(came, keep.shape[0]), first // BLK)
    key = turn(whole[:, :HW], ropes[:, :HW], ropes[:, HW:]).astype(BF16)
    value = whole[:, HW:].astype(BF16)
    latest[:, :HW] = key
    latest[:, HW:] = value

    def wide(rows):
        return jnp.broadcast_to(rows[:, None, :], (comps, group, HW)).reshape(comps * group, HW)

    slot = lax.broadcasted_iota(jnp.int32, (group, HW), 1)
    for c in range(comps):
        span = slice(c * group, (c + 1) * group)
        score = nt(turned[span, :].astype(BF16), cache[c, :, :HW]) * scale
        scores[span, :] = jnp.where(slot < lengths[c], score, NEG)
    own_score = jnp.sum(turned[...] * wide(key.astype(F32)), axis=1, keepdims=True) * scale
    masked = scores[...]
    top = jnp.maximum(jnp.max(masked, axis=1, keepdims=True), own_score)
    weight = jnp.exp(masked - top)
    own_weight = jnp.exp(own_score - top)
    total = jnp.sum(weight, axis=1, keepdims=True) + own_weight
    weights[...] = weight
    for c in range(comps):
        span = slice(c * group, (c + 1) * group)
        out[span, :] = nn(weights[span, :].astype(BF16), cache[c, :, HW:])
    out[...] = out[...] + own_weight.astype(BF16).astype(F32) * wide(value.astype(F32))
    lane = lax.broadcasted_iota(jnp.int32, stats.shape, 1)
    stats[...] = jnp.where(lane < HW // 2, top, total)


def suffix(lengths, turned, cache, came, keep, bias, ropes):
    comps = ropes.shape[0]
    rows = turned.shape[0]
    vmem = pl.BlockSpec(memory_space=pltpu.VMEM)
    return pl.pallas_call(
        suffix_body,
        in_specs=[pl.BlockSpec(memory_space=pltpu.SMEM)] + [vmem] * 6,
        out_shape=[
            jax.ShapeDtypeStruct((comps, 2 * HW), BF16),
            jax.ShapeDtypeStruct((rows, HW), F32),
            jax.ShapeDtypeStruct((rows, HW), F32),
        ],
        scratch_shapes=[pltpu.VMEM((rows, HW), F32), pltpu.VMEM((rows, HW), F32), pltpu.VMEM((comps, 2 * HW), F32)],
        compiler_params=pltpu.CompilerParams(vmem_limit_bytes=LIMIT),
        cost_estimate=pl.CostEstimate(flops=10**7, bytes_accessed=10**7, transcendentals=0),
        name="suffix",
    )(lengths, turned, cache, came, keep, bias, ropes)


def prefix_body(queries, bias, turns, *refs):
    chunks = len(PARTS)
    came, keep = refs[:chunks], refs[chunks : 2 * chunks]
    kv, out = refs[2 * chunks :]
    blocks = kv.shape[0] // BLK
    cos_in, sin_in = turns[blocks:, :HW], turns[blocks:, HW:]
    for i, (first, rows) in enumerate(PARTS):
        scale = scales(came[i], keep[i].shape[0])
        for k in range(rows // BLK):
            span = slice(first + k * BLK, first + (k + 1) * BLK)
            total = keep[i][k * BLK : (k + 1) * BLK, :] + decode(came[i], scale, k) + bias[...]
            at = first // BLK + k
            cos_at, sin_at = turns[at : at + 1, :HW], turns[at : at + 1, HW:]
            cosine, sine = cos_at * cos_in - sin_at * sin_in, sin_at * cos_in + cos_at * sin_in
            kv[span, :HW] = turn(total[:, :HW], cosine, sine).astype(BF16)
            kv[span, HW:] = total[:, HW:].astype(BF16)
    prompts, per, _ = queries.shape
    step = 16
    for s in range(0, prompts, step):
        q = queries[s : s + step].reshape(step * per, HW)
        scores = nt(q, kv[:, :HW]) * (HW ** -0.5)
        top = jnp.max(scores, axis=1, keepdims=True)
        weight = jnp.exp(scores - top)
        total = jnp.sum(weight, axis=1, keepdims=True)
        part = nn(weight.astype(BF16), kv[:, HW:])
        peak = jnp.maximum(jnp.max(jnp.abs(part), axis=1, keepdims=True), 1e-30)
        level = jnp.ceil(jnp.log2(peak) * 256.0) + 1.0
        code = near_int(part * (jnp.exp2(level * (-1.0 / 256.0)) * QMAX))
        lane = lax.broadcasted_iota(jnp.int32, (step * per, HW), 1)
        row = lax.broadcasted_iota(jnp.int32, (step * per, HW), 0) % per
        stat = jnp.zeros((step * per, HW), F32)
        for i, piece in enumerate(pieces(top, TOP_STEPS) + pieces(total, TOTAL_STEPS) + [level]):
            stat = stat + jnp.where(lane == row + i * per, piece, 0.0)
        stat = jnp.sum(stat.reshape(step, per, HW), axis=1, keepdims=True)
        whole = jnp.concatenate([code.reshape(step, per, HW), jnp.broadcast_to(stat, (step, 8, HW))], axis=1)
        out[s : s + step] = whole.astype(jnp.int32).astype(jnp.int16)


def prefix(queries, bias, turns, came, keep, length):
    prompts, per, _ = queries.shape
    return pl.pallas_call(
        prefix_body,
        out_shape=[
            jax.ShapeDtypeStruct((length, 2 * HW), BF16),
            jax.ShapeDtypeStruct((prompts, per + 8, HW), jnp.int16),
        ],
        compiler_params=pltpu.CompilerParams(vmem_limit_bytes=LIMIT),
        cost_estimate=pl.CostEstimate(flops=2 * 10**8, bytes_accessed=10**7, transcendentals=10**6),
        name="prefix",
    )(queries, bias, turns, *came, *keep)


def merge_body(place, back, out, stats, attn, spread, side, joined):
    prompts, per, _ = back.shape
    per -= 8
    rows = out.shape[0]
    comps = attn.shape[0]
    group = rows // comps
    came = back[...].astype(jnp.int32).astype(F32)
    spread[...] = came
    for c in range(comps):
        at = place[c]
        span = slice(c * group, (c + 1) * group)
        slot = at % 2
        joined[span, :] = spread[at // 2, pl.ds(pl.multiple_of(slot * group, group), group), :]
        side[span, :] = jnp.where(
            lax.broadcasted_iota(jnp.int32, (group, HW), 1) % per
            == lax.broadcasted_iota(jnp.int32, (group, HW), 0) + slot * group,
            spread[at // 2, per:, :], 0.0)
    lane = lax.broadcasted_iota(jnp.int32, (rows, HW), 1)
    stat = []
    for i in range(len(TOP_STEPS) + len(TOTAL_STEPS) + 1):
        stat.append(jnp.sum(jnp.where(lane // per == i, side[...], 0.0), axis=1, keepdims=True))
    top_p = sum(piece * step for piece, step in zip(stat, TOP_STEPS))
    total_p = sum(piece * step for piece, step in zip(stat[len(TOP_STEPS) :], TOTAL_STEPS))
    out_p = joined[...] * (jnp.exp2(stat[-1] * (1.0 / 256.0)) * (1.0 / QMAX))
    top_s, total_s = stats[:, :1], stats[:, HW // 2 : HW // 2 + 1]
    top = jnp.maximum(top_p, top_s)
    alpha = jnp.exp(top_p - top)
    beta = jnp.exp(top_s - top)
    joined[...] = (alpha * out_p + beta * out[...]) / (alpha * total_p + beta * total_s)
    for h in range(group):
        attn[:, h * HW : (h + 1) * HW] = joined[pl.ds(h, comps, stride=group), :].astype(BF16)


def merge(place, back, out, stats, comps):
    rows = out.shape[0]
    vmem = pl.BlockSpec(memory_space=pltpu.VMEM)
    smem = pl.BlockSpec(memory_space=pltpu.SMEM)
    return pl.pallas_call(
        merge_body,
        in_specs=[smem, vmem, vmem, vmem],
        out_specs=vmem,
        out_shape=jax.ShapeDtypeStruct((comps, rows // comps * HW), BF16),
        scratch_shapes=[pltpu.VMEM(back.shape, F32), pltpu.VMEM((rows, HW), F32), pltpu.VMEM((rows, HW), F32)],
        compiler_params=pltpu.CompilerParams(vmem_limit_bytes=LIMIT),
        cost_estimate=pl.CostEstimate(flops=10**6, bytes_accessed=10**6, transcendentals=10**5),
        name="merge",
    )(place, back, out, stats)


def on_device(
    prefix_hidden_states, latest_hidden, queries, suffix_key_cache, key_value_weight, key_value_bias,
    adapter_down_weight, adapter_up_weight, parents, adapter_index, suffix_length_count,
):
    length = prefix_hidden_states.shape[1]
    comps = latest_hidden.shape[0]
    prompts = adapter_index.shape[0]
    along_y = lambda d: [(a * 2 + b, ((a + d) % 4) * 2 + b) for a in range(4) for b in range(2)]
    along_z = [(a * 2 + b, a * 2 + 1 - b) for a in range(4) for b in range(2)]

    hidden = prefix_hidden_states[0]
    y_step = lambda value, d: lax.ppermute(value, "tp", along_y(d))
    parent = parents[:, 0]
    in_hbm = lambda value: pltpu.with_memory_space_constraint(value, pltpu.HBM)
    hidden, key_value_weight, adapter_down_weight, adapter_up_weight, latest_hidden = map(
        in_hbm, (hidden, key_value_weight, adapter_down_weight, adapter_up_weight, latest_hidden))
    adapter_index, parent = in_hbm(adapter_index), in_hbm(parent)
    inputs = (adapter_index, parent, hidden, key_value_weight, adapter_down_weight, adapter_up_weight, latest_hidden)
    far0, far1, *known = project_far(FAR_LIMIT, *inputs)
    far0, far1 = y_step(far0, 1), y_step(far1, -1)
    direct0, direct1, near0, near1, own0, own1 = project_near(NEAR_LIMIT, *inputs, known)
    direct0, queries = lax.optimization_barrier((direct0, queries))

    cos_t, sin_t = rope_tables(length + 1, suffix_key_cache.shape[1])
    table = jnp.asarray(np.concatenate([cos_t, sin_t], 1))
    to_prompts, turned, ropes, place = dispatch(parent, suffix_length_count, queries, table, prompts)
    near0, near1, to_prompts = lax.optimization_barrier((near0, near1, to_prompts))
    joined0, joined1 = relay(far0, near0), relay(far1, near1)
    joined1, to_prompts = lax.optimization_barrier((joined1, to_prompts))
    joined0, direct0 = y_step(joined0, 1), y_step(direct0, -1)
    joined1, direct1 = y_step(joined1, -1), y_step(direct1, 1)
    here = lax.all_to_all(to_prompts, "rep", 0, 0, tiled=True)
    code0, keep0 = fold(joined0, direct0, own0)
    came0 = lax.ppermute(code0, "tp", along_z)
    code1, keep1 = fold(joined1, direct1, own1)
    came1 = lax.ppermute(code1, "tp", along_z)
    came, keep = (came0, came1), (keep0, keep1)

    bias = key_value_bias.astype(F32).reshape(1, 2 * HW)
    latest_key_value, out_s, stats = suffix(
        suffix_length_count, turned, in_hbm(suffix_key_cache), came[1], keep[1], bias, ropes)
    blocks, within = rope_tables(0, length, BLK), rope_tables(0, BLK)
    turns = jnp.asarray(np.concatenate([np.concatenate(blocks, 1), np.concatenate(within, 1)], 0))
    prefix_kv, part = prefix(here, bias, in_hbm(turns), came, keep, length)
    back = lax.all_to_all(part, "rep", 0, 0, tiled=True)
    attn_out = merge(place, back, out_s, stats, comps)
    return prefix_kv[None], latest_key_value, attn_out


def solution(mesh):
    in_specs = (
        P("rep", None, "tp"), P("rep", "tp"), P("rep", "tp"), P("rep", None, "tp"), P("tp", None), P("tp"),
        P("tp", None), P(), P("rep", None), P(), P("rep"),
    )
    out_specs = (P("rep", None, "tp"), P("rep", "tp"), P("rep", "tp"))
    return jax.shard_map(on_device, mesh=mesh, in_specs=in_specs, out_specs=out_specs, check_vma=False)
```
